256 devices in a mesh: dp: 2 (over core), ctx: 32 (over z, x), head: 4 (over y).
Axes of the slice: x: 4, y: 4, z: 8, core: 2. Of those that a mesh axis runs over, the one named last changes fastest.
Arguments:
- query_rows: bfloat16 [4096, 3072], P(('dp', 'ctx', 'head')), parts along dimension 0, may hold values from -6 to 6
- key_rows: bfloat16 [16384, 512], P(('dp', 'ctx'), 'head'), parts along dimension 0, may hold values from -6 to 6
- value_rows: bfloat16 [16384, 512], P(('dp', 'ctx'), 'head'), parts along dimension 0, may hold values from -6 to 6
- output_rows: bfloat16 [4096, 3072], P(('dp', 'ctx', 'head')), parts along dimension 0, may hold values from -1.5 to 1.5
- grad_out: bfloat16 [4096, 3072], P(('dp', 'ctx', 'head')), parts along dimension 0, may hold values from -768 to 768
- log_norm: float32 [4096, 24], P(('dp', 'ctx', 'head')), parts along dimension 0
- mask_table: int32 [32, 5], P('dp'), parts along dimension 0, may hold values from 0 to 8192, as said below
- key_order: int32 [256], P('dp'), parts along dimension 0, may hold values from 0 to 127, each once
- query_order: int32 [256], P('dp'), parts along dimension 0, may hold values from 0 to 127, each once
Outputs:
- grad_query: bfloat16 [4096, 3072], P(('dp', 'ctx', 'head')), parts along dimension 0
- grad_key: bfloat16 [16384, 512], P(('dp', 'ctx'), 'head'), parts along dimension 0
- grad_value: bfloat16 [16384, 512], P(('dp', 'ctx'), 'head'), parts along dimension 0
The draws below stay inside these ranges and needn't reach their ends.
There are 2 independent parts, one for each index of `dp`. The reference program is written for one: setup_inputs(seed, part) draws one part's arguments, and reference() takes and returns one part's arrays. A program takes and returns all parts, laid end to end along the dimension named above; each array names one. Nothing has to cross between parts.
Inputs may be any that keep to these rules, and one draw needn't show every extreme that they name: `mask_table`: row s covers the slab positions 6144 + s * 128 (column 0) up to 6144 + (s + 1) * 128 (column 1, exclusive); column 3 equals column 1; column 2 is at most column 0; column 4 is 0 (every key in the range allowed) or 1 (only keys at or before the query's own position); the last row has kind 0. `key_order`: each stretch number appears once. `query_order`: each stretch number appears once.
All inputs are finite; a program needn't handle non-finite values.
Results may differ from the reference program's by a relative error of at most 0.0053.
Values may be sent and summed in bfloat16 or wider, within the bound.
A program may use at most 64 MiB of HBM per device.

```python
import math
import jax
import jax.numpy as jnp
from jax import lax

HEADS = 24
KV_HEADS = 4
HEAD_DIM = 128
BLOCK = 128
KEYS = 8192
QUERIES = 2048
SLICES = 16
STRETCHES = 128
KCHUNK = 64
QCHUNK = 16


def draw_log_norm(key, part):
    key = jax.random.fold_in(key, 7)
    centre = jnp.log(jnp.float32(KEYS)) + 0.5
    spread = jax.random.uniform(key, (QUERIES, HEADS), jnp.float32, -1.0, 1.0)
    return centre + spread


def draw_mask_table(key, part):
    key = jax.random.fold_in(key, 11)
    start_key, kind_key, reach_key = jax.random.split(key, 3)
    clip_start = jax.random.randint(start_key, (), 0, KEYS // 3 + 1)
    positions = jnp.arange(SLICES, dtype=jnp.int32)
    textual = (jax.random.randint(kind_key, (SLICES,), 0, 4) == 0) & (positions < SLICES - 1)
    reach = jax.random.randint(reach_key, (SLICES,), 0, BLOCK)
    query_low = KEYS - QUERIES + positions * BLOCK
    query_high = query_low + BLOCK
    key_low = jnp.where(textual, query_low - reach, clip_start)
    slice_kind = textual.astype(jnp.int32)
    return jnp.stack([query_low, query_high, key_low, query_high, slice_kind], axis=1).astype(jnp.int32)


def block_scale(rng, extent, pieces, least, high):
    level, own = 1.0, jax.random.fold_in(rng, 6)
    for dim, shards_of in pieces:
        heights = jnp.exp(jax.random.uniform(jax.random.fold_in(own, dim), (shards_of,), jnp.float32, least / len(pieces), high / len(pieces)))
        level = level * jnp.repeat(heights, extent[dim] // shards_of).reshape([-1 if axis == dim else 1 for axis in range(len(extent))])
    return level


def noise(key, dims, deviation, most, shards=(), held_as=jnp.bfloat16):
    result = jax.random.normal(key, dims, jnp.float32) * deviation
    if len(shards) > 0:
        result = block_scale(key, dims, shards, -0.22, 0.18) * result
    return jnp.clip(result, min=-most, max=most).astype(held_as)


def setup_inputs(seed: int = 0, part: int = 0) -> dict:
    streams_of = jax.random.split(jax.random.key(seed), 10)
    own_keys = jax.random.split(jax.random.fold_in(streams_of[9], part), 10)
    query_rows = noise(own_keys[0], (QUERIES, HEADS * HEAD_DIM), 1.0, 6.0, ((0, 128),))
    key_rows = noise(own_keys[1], (KEYS, KV_HEADS * HEAD_DIM), 1.0, 6.0, ((0, 32), (1, 4)))
    value_rows = noise(own_keys[2], (KEYS, KV_HEADS * HEAD_DIM), 1.0, 6.0, ((0, 32), (1, 4)))
    output_rows = noise(own_keys[3], (QUERIES, HEADS * HEAD_DIM), 0.25, 1.5, ((0, 128),))
    grad_out = noise(own_keys[4], (QUERIES, HEADS * HEAD_DIM), (KEYS // 64), 768.0, ((0, 128),))
    log_norm = draw_log_norm(jax.random.fold_in(jax.random.fold_in(streams_of[9], part), 71), part)
    mask_table = draw_mask_table(jax.random.fold_in(jax.random.fold_in(streams_of[9], part), 71), part)
    key_order = jax.random.permutation(own_keys[7], STRETCHES).astype(jnp.int32)
    query_order = jax.random.permutation(own_keys[8], STRETCHES).astype(jnp.int32)
    return {"query_rows": query_rows, "key_rows": key_rows, "value_rows": value_rows, "output_rows": output_rows, "grad_out": grad_out, "log_norm": log_norm, "mask_table": mask_table, "key_order": key_order, "query_order": query_order}


def stretch_positions(stretch_order, stretch_width, offset):
    within = jnp.arange(stretch_width, dtype=jnp.int32)
    return offset + (stretch_order[:, None] * stretch_width + within[None, :]).reshape(-1)

def slice_bounds(query_pos, mask_table):
    inside = ((query_pos[:, None] >= mask_table[None, :, 0]) & (query_pos[:, None] < mask_table[None, :, 1])).astype(jnp.int32)
    key_low = lax.optimization_barrier(jnp.sum(inside * mask_table[None, :, 2], axis=1))
    key_high = lax.optimization_barrier(jnp.sum(inside * mask_table[None, :, 3], axis=1))
    causal = lax.optimization_barrier(jnp.sum(inside * mask_table[None, :, 4], axis=1))
    return (key_low, key_high, causal)

def allowed_pairs(query_pos, key_low, key_high, causal, key_pos):
    key_grid = key_pos[None, :]
    return (key_grid >= key_low[:, None]) & (key_grid < key_high[:, None]) & ((causal[:, None] == 0) | (key_grid <= query_pos[:, None]))

def reference(query_rows, key_rows, value_rows, output_rows, grad_out, log_norm, mask_table, key_order, query_order):
    score_scale = 1.0 / math.sqrt(HEAD_DIM)
    group = HEADS // KV_HEADS
    key_pos = stretch_positions(key_order, KCHUNK, 0)
    query_pos = stretch_positions(query_order, QCHUNK, KEYS - QUERIES)
    key_low, key_high, causal = slice_bounds(query_pos, mask_table)
    allowed = allowed_pairs(query_pos, key_low, key_high, causal, key_pos)

    def by_head(matrix, row_total, head_total):
        return matrix.reshape(row_total, head_total, HEAD_DIM).transpose(1, 0, 2)
    delta_rows = lax.optimization_barrier(jnp.sum(by_head(grad_out, QUERIES, HEADS).astype(jnp.float32) * by_head(output_rows, QUERIES, HEADS).astype(jnp.float32), axis=2))

    def grouped(stacked):
        return stacked.reshape((KV_HEADS, group) + stacked.shape[1:])

    def one_kv(operands):
        key_head, value_head, query_group, grad_group, norm_group, delta_group = operands

        def one_query_head(totals, inner):
            query_head, grad_head, norm_head, delta_head = inner
            scores = jnp.dot(query_head, key_head.T, preferred_element_type=jnp.float32) * score_scale
            weights = jnp.where(allowed, jnp.exp(scores - norm_head[:, None]), jnp.float32(0.0))
            dprobs = jnp.dot(grad_head, value_head.T, preferred_element_type=jnp.float32)
            dscore = (weights * (dprobs - delta_head[:, None])).astype(jnp.bfloat16)
            grad_query_head = (jnp.dot(dscore, key_head, preferred_element_type=jnp.float32) * score_scale).astype(jnp.bfloat16)
            key_total = totals[0] + jnp.dot(dscore.T, query_head, preferred_element_type=jnp.float32)
            value_total = totals[1] + jnp.dot(weights.astype(jnp.bfloat16).T, grad_head, preferred_element_type=jnp.float32)
            return ((key_total, value_total), grad_query_head)
        zeros_rows = jnp.zeros((KEYS, HEAD_DIM), jnp.float32)
        totals, grad_query_group = lax.scan(one_query_head, (zeros_rows, zeros_rows), (query_group, grad_group, norm_group, delta_group))
        return (grad_query_group, (totals[0] * score_scale).astype(jnp.bfloat16), totals[1].astype(jnp.bfloat16))
    stacked_query, stacked_key, stacked_value = lax.map(one_kv, (by_head(key_rows, KEYS, KV_HEADS), by_head(value_rows, KEYS, KV_HEADS), grouped(by_head(query_rows, QUERIES, HEADS)), grouped(by_head(grad_out, QUERIES, HEADS)), grouped(log_norm.T), grouped(delta_rows)))

    def back_rows(stacked, row_total, head_total):
        return stacked.reshape(head_total, row_total, HEAD_DIM).transpose(1, 0, 2).reshape(row_total, head_total * HEAD_DIM)
    return (back_rows(stacked_query, QUERIES, HEADS), back_rows(stacked_key, KEYS, KV_HEADS), back_rows(stacked_value, KEYS, KV_HEADS))
```

```python
import functools
import math

import jax
import jax.numpy as jnp
from jax import lax
from jax.experimental import pallas as pl
from jax.experimental.pallas import tpu as pltpu
from jax.sharding import PartitionSpec as P

HEAD_DIM = 128
DISPATCH = 4
KCHUNK = 64
QCHUNK = 16
RING_X = 4
MESH = pl.DeviceIdType.MESH
F32 = jnp.float32
BF16 = jnp.bfloat16


def dot_nt(lhs, rhs):
    return lax.dot_general(lhs, rhs, (((1,), (1,)), ((), ())), preferred_element_type=F32)


def dot_nn(lhs, rhs):
    return lax.dot_general(lhs, rhs, (((1,), (0,)), ((), ())), preferred_element_type=F32)


def dot_tn(lhs, rhs):
    return lax.dot_general(lhs, rhs, (((0,), (0,)), ((), ())), preferred_element_type=F32)


def kernel(
    sizes,
    q_hbm,
    k_hbm,
    v_hbm,
    o_hbm,
    g_hbm,
    norm_hbm,
    table,
    key_order,
    query_order,
    dq_out,
    dk_out,
    dv_out,
    q_all,
    g_all,
    nd_all,
    k_all,
    v_all,
    q_own,
    o_own,
    g_own,
    norm_own,
    nd_own,
    nd_rows,
    bias,
    dq_acc,
    dq_send,
    dq_recv,
    part_k,
    part_v,
    chain_send,
    chain_recv,
    load_sem,
    plane_send,
    plane_recv,
    ring_send,
    ring_recv,
    chain_send_sem,
    chain_recv_sem,
    dq_send_sem,
    dq_recv_sem,
):
    size_z, size_x, size_y = sizes
    half = size_z // 2
    plane = size_x * size_y
    rows = plane * QCHUNK
    key_count = k_hbm.shape[0]
    heads_all = norm_hbm.shape[1]
    heads_loc = heads_all // size_y
    width = heads_loc * HEAD_DIM
    score_scale = 1.0 / math.sqrt(HEAD_DIM)
    log2e = math.log2(math.e)

    ctx = lax.axis_index("ctx")
    my_y = lax.axis_index("head")
    my_z = ctx // size_x
    my_x = ctx % size_x
    me = my_x * size_y + my_y
    my_rows = pl.ds(pl.multiple_of(me * QCHUNK, QCHUNK), QCHUNK)
    my_cols = pl.ds(pl.multiple_of(my_y * width, 128), width)

    def ring_z(offset):
        return (my_z + offset + size_z) % size_z

    def z_device(offset):
        return {"ctx": ring_z(offset) * size_x + my_x, "head": my_y}

    def plane_peer(dx, dy):
        px = (my_x + dx) % size_x
        py = (my_y + dy) % size_y
        return px, py, {"ctx": my_z * size_x + px, "head": py}

    peers = [(dx, dy) for dx in range(size_x) for dy in range(size_y) if dx or dy]
    peers.sort(key=lambda p: -(min(p[0], size_x - p[0]) + min(p[1], size_y - p[1])))

    own_k = k_all.at[my_z]
    own_v = v_all.at[my_z]
    loads = [
        pltpu.make_async_copy(k_hbm, own_k, load_sem.at[0]),
        pltpu.make_async_copy(v_hbm, own_v, load_sem.at[1]),
        pltpu.make_async_copy(g_hbm, g_own, load_sem.at[2]),
        pltpu.make_async_copy(o_hbm, o_own, load_sem.at[3]),
        pltpu.make_async_copy(norm_hbm, norm_own, load_sem.at[4]),
        pltpu.make_async_copy(q_hbm, q_own, load_sem.at[5]),
    ]
    for copy in loads:
        copy.start()

    barrier = pltpu.get_barrier_semaphore()
    for offset in (1, -1):
        pl.semaphore_signal(barrier, inc=1, device_id=z_device(offset), device_id_type=MESH)
    for dx, dy in peers:
        _, _, target = plane_peer(dx, dy)
        pl.semaphore_signal(barrier, inc=1, device_id=target, device_id_type=MESH)

    for copy in loads:
        copy.wait()

    lane = lax.broadcasted_iota(jnp.int32, (QCHUNK, 128), 1)
    tile = jnp.zeros((QCHUNK, 128), F32)
    for head in range(heads_all):
        cols = pl.ds(head * HEAD_DIM, HEAD_DIM)
        delta = jnp.sum(
            g_own[:, cols].astype(F32) * o_own[:, cols].astype(F32), axis=1, keepdims=True
        )
        tile = jnp.where(lane == heads_all + head, delta, tile)
    nd_own[...] = tile
    nd_own[:, 0:heads_all] = norm_own[...] * log2e

    pl.semaphore_wait(barrier, len(peers) + 2)

    def ring_copy(ref, way, step, index):
        slot = ring_z(-way * (step - 1))
        return pltpu.make_async_remote_copy(
            src_ref=ref.at[slot],
            dst_ref=ref.at[slot],
            send_sem=ring_send.at[index],
            recv_sem=ring_recv.at[index],
            device_id=z_device(way),
            device_id_type=MESH,
        )

    ring_plan = []
    for ref, way, steps in (
        (k_all, 1, half),
        (v_all, -1, half),
        (v_all, 1, half - 1),
        (k_all, -1, half - 1),
    ):
        ring_plan.append((ref, way, steps))
    ring = {}
    count = 0
    for step in range(1, half + 1):
        for line, (ref, way, steps) in enumerate(ring_plan):
            if step <= steps:
                ring[(line, step)] = ring_copy(ref, way, step, count)
                count += 1
    for line in range(4):
        if (line, 1) in ring:
            ring[(line, 1)].start()

    for slot, (dx, dy) in enumerate(peers):
        px, py, target = plane_peer(dx, dy)
        cols = pl.ds(pl.multiple_of(py * width, 128), width)
        for kind, (src, dst) in enumerate(
            ((nd_own, nd_all), (q_own.at[:, cols], q_all), (g_own.at[:, cols], g_all))
        ):
            pltpu.make_async_remote_copy(
                src_ref=src,
                dst_ref=dst.at[my_rows],
                send_sem=plane_send.at[kind],
                recv_sem=plane_recv.at[kind],
                device_id=target,
                device_id_type=MESH,
            ).start()
    pltpu.make_async_copy(nd_own, nd_all.at[my_rows], plane_recv.at[0]).start()
    pltpu.make_async_copy(q_own.at[:, my_cols], q_all.at[my_rows], plane_recv.at[1]).start()
    pltpu.make_async_copy(g_own.at[:, my_cols], g_all.at[my_rows], plane_recv.at[2]).start()

    qlane = lax.broadcasted_iota(jnp.int32, (1, rows), 1)
    qpos = jnp.zeros((1, rows), jnp.int32)
    for chunk in range(plane):
        qpos = jnp.where(qlane // QCHUNK == chunk, query_order[my_z * plane + chunk], qpos)
    offset = key_order.shape[0] * KCHUNK - query_order.shape[0] * QCHUNK
    qpos = offset + qpos * QCHUNK + qlane % QCHUNK
    low = jnp.zeros((1, rows), jnp.int32)
    high = jnp.zeros((1, rows), jnp.int32)
    for row in range(table.shape[0]):
        inside = (qpos >= table[row, 0]) & (qpos < table[row, 1])
        last = jnp.where(table[row, 4] != 0, jnp.minimum(table[row, 3], qpos + 1), table[row, 3])
        low = jnp.where(inside, table[row, 2], low)
        high = jnp.where(inside, last, high)
    krow = lax.broadcasted_iota(jnp.int32, (KCHUNK, rows), 0)
    dq_acc[...] = jnp.zeros_like(dq_acc)

    for step in range(2, half + 1):
        for line in range(4):
            if (line, step - 1) in ring:
                ring[(line, step - 1)].wait_recv()
            if (line, step) in ring:
                ring[(line, step)].start()

    for kind, dst in enumerate((nd_all, q_all, g_all)):
        pltpu.make_async_copy(dst, dst, plane_recv.at[kind]).wait()
    turned = nd_all[...].T
    nd_rows[...] = turned[0 : 2 * heads_all]

    order = [0, 1, -1, half]
    for distance in range(half - 1, 1, -1):
        order += [distance, -distance]

    def block_terms(index, dist):
        zb = ring_z(dist)
        first = (zb * size_x + my_x) * DISPATCH
        for part in range(DISPATCH):
            base = key_order[first + part] * KCHUNK
            ok = (krow >= low - base) & (krow < high - base)
            bias[pl.ds(part * KCHUNK, KCHUNK), :] = jnp.where(ok, jnp.inf, -jnp.inf).astype(F32)
        key_blk = k_all[zb]
        value_blk = v_all[zb]
        dk = jnp.zeros((key_count, HEAD_DIM), F32)
        dv = jnp.zeros((key_count, HEAD_DIM), F32)
        for head in range(heads_loc):
            cols = pl.ds(head * HEAD_DIM, HEAD_DIM)
            qh = q_all[:, cols]
            gh = g_all[:, cols]
            norm = nd_rows[pl.ds(my_y * heads_loc + head, 1), :]
            delta = nd_rows[pl.ds(heads_all + my_y * heads_loc + head, 1), :]
            scores = dot_nt(key_blk, qh)
            weights = jnp.exp2(jnp.minimum(scores * (score_scale * log2e) - norm, bias[...]))
            dprobs = dot_nt(value_blk, gh)
            dscore = (weights * (dprobs - delta)).astype(BF16)
            dv += dot_nn(weights.astype(BF16), gh)
            dk += dot_nn(dscore, qh)
            dq_acc[:, cols] += dot_tn(dscore, key_blk)
        part_k[index] = dk
        part_v[index] = dv

    lines = {("k", 1): half, ("v", -1): half, ("v", 1): half - 1, ("k", -1): half - 1}
    slots = {}
    for (kind, way), first_dist in lines.items():
        for dist in range(first_dist, 0, -1):
            slots[(kind, way, dist)] = len(slots)

    def chain_copy(kind, way, dist):
        slot = slots[(kind, way, dist)]
        return pltpu.make_async_remote_copy(
            src_ref=chain_send.at[slot],
            dst_ref=chain_recv.at[slot],
            send_sem=chain_send_sem.at[slot],
            recv_sem=chain_recv_sem.at[slot],
            device_id=z_device(way),
            device_id_type=MESH,
        )

    def chain_step(kind, way, dist):
        if (kind, way, dist) not in slots:
            return
        index = order.index(half if dist == half else way * dist)
        value = (part_k if kind == "k" else part_v)[index]
        if dist < lines[(kind, way)]:
            chain_copy(kind, way, dist + 1).wait_recv()
            value = value + chain_recv[slots[(kind, way, dist + 1)]].astype(F32)
        chain_send[slots[(kind, way, dist)]] = value.astype(BF16)
        chain_copy(kind, way, dist).start()

    def dist_at(index):
        later = index - 4
        far = half - 1 - later // 2
        return jnp.where(
            index == 0,
            0,
            jnp.where(
                index == 1,
                1,
                jnp.where(
                    index == 2,
                    -1,
                    jnp.where(index == 3, half, jnp.where(later % 2 == 0, far, -far)),
                ),
            ),
        )

    def block_step(index, carry):
        @pl.when(index == 3)
        def _():
            for line in range(4):
                if ring_plan[line][2] == half:
                    ring[(line, half)].wait_recv()

        block_terms(index, dist_at(index))

        for at in range(3, size_z):
            dist = order[at]

            @pl.when(index == at)
            def _(dist=dist):
                if dist == half:
                    chain_step("k", 1, half)
                    chain_step("v", -1, half)
                elif dist > 0:
                    chain_step("v", 1, dist)
                else:
                    chain_step("k", -1, -dist)
                    chain_step("k", 1, -dist)
                    chain_step("v", -1, -dist)

        return carry

    lax.fori_loop(0, size_z, block_step, 0)

    dq_send[...] = dq_acc[...].astype(BF16)
    for dx, dy in peers:
        px, py, target = plane_peer(dx, dy)
        peer_rows = pl.ds(pl.multiple_of((px * size_y + py) * QCHUNK, QCHUNK), QCHUNK)
        pltpu.make_async_remote_copy(
            src_ref=dq_send.at[peer_rows],
            dst_ref=dq_recv.at[my_x, :, my_cols],
            send_sem=dq_send_sem,
            recv_sem=dq_recv_sem,
            device_id=target,
            device_id_type=MESH,
        ).start()
    pltpu.make_async_copy(
        dq_send.at[my_rows], dq_recv.at[my_x, :, my_cols], dq_recv_sem
    ).start()

    chain_step("v", 1, 1)
    chain_step("k", -1, 1)
    chain_step("k", 1, 1)
    chain_step("v", -1, 1)

    pltpu.make_async_copy(dq_recv, dq_recv, dq_recv_sem).wait()
    total = dq_recv[0].astype(F32)
    for other in range(1, size_x):
        total = total + dq_recv[other].astype(F32)
    dq_out[...] = (total * score_scale).astype(BF16)

    for kind, part, out, scale in (("v", part_v, dv_out, 1.0), ("k", part_k, dk_out, score_scale)):
        value = part[0]
        for way in (1, -1):
            if (kind, way, 1) in slots:
                chain_copy(kind, way, 1).wait_recv()
                value = value + chain_recv[slots[(kind, way, 1)]].astype(F32)
        out[...] = (value * scale).astype(BF16)

    for copy in ring.values():
        copy.wait_send()
    for key in slots:
        chain_copy(*key).wait_send()
    sent = pl.ds(0, len(peers) * QCHUNK)
    for kind, dst in enumerate((nd_all, q_all, g_all)):
        pltpu.make_async_copy(dst.at[sent], dst.at[sent], plane_send.at[kind]).wait()
    pltpu.make_async_copy(dq_send.at[sent], dq_send.at[sent], dq_send_sem).wait()


def local(
    sizes,
    query_rows,
    key_rows,
    value_rows,
    output_rows,
    grad_out,
    log_norm,
    mask_table,
    key_order,
    query_order,
):
    size_z, size_x, size_y = sizes
    half = size_z // 2
    rows = size_x * size_y * QCHUNK
    key_count = key_rows.shape[0]
    own, columns = query_rows.shape
    heads_all = log_norm.shape[1]
    width = columns // size_y
    chain = 2 * (2 * half - 1)
    hbm = pl.BlockSpec(memory_space=pl.ANY)
    smem = pl.BlockSpec(memory_space=pltpu.SMEM)
    vmem = pl.BlockSpec(memory_space=pltpu.VMEM)
    dma = pltpu.SemaphoreType.DMA
    return pl.pallas_call(
        functools.partial(kernel, sizes),
        out_shape=(
            jax.ShapeDtypeStruct(query_rows.shape, BF16),
            jax.ShapeDtypeStruct(key_rows.shape, BF16),
            jax.ShapeDtypeStruct(value_rows.shape, BF16),
        ),
        in_specs=[hbm] * 6 + [smem] * 3,
        out_specs=(vmem, vmem, vmem),
        scratch_shapes=[
            pltpu.VMEM((rows, width), BF16),
            pltpu.VMEM((rows, width), BF16),
            pltpu.VMEM((rows, 128), F32),
            pltpu.VMEM((size_z, key_count, HEAD_DIM), BF16),
            pltpu.VMEM((size_z, key_count, HEAD_DIM), BF16),
            pltpu.VMEM((own, columns), BF16),
            pltpu.VMEM((own, columns), BF16),
            pltpu.VMEM((own, columns), BF16),
            pltpu.VMEM((own, heads_all), F32),
            pltpu.VMEM((own, 128), F32),
            pltpu.VMEM((2 * heads_all, rows), F32),
            pltpu.VMEM((key_count, rows), F32),
            pltpu.VMEM((rows, width), F32),
            pltpu.VMEM((rows, width), BF16),
            pltpu.VMEM((size_x, own, columns), BF16),
            pltpu.VMEM((size_z, key_count, HEAD_DIM), F32),
            pltpu.VMEM((size_z, key_count, HEAD_DIM), F32),
            pltpu.VMEM((chain, key_count, HEAD_DIM), BF16),
            pltpu.VMEM((chain, key_count, HEAD_DIM), BF16),
            dma((6,)),
            dma((3,)),
            dma((3,)),
            dma((chain,)),
            dma((chain,)),
            dma((chain,)),
            dma((chain,)),
            dma,
            dma,
        ],
        compiler_params=pltpu.CompilerParams(
            collective_id=0, has_side_effects=True, vmem_limit_bytes=32 * 1024 * 1024
        ),
    )(
        query_rows,
        key_rows,
        value_rows,
        output_rows,
        grad_out,
        log_norm,
        mask_table,
        key_order,
        query_order,
    )


def solution(mesh, ring_x=RING_X):
    sizes = (mesh.shape["ctx"] // ring_x, ring_x, mesh.shape["head"])
    return jax.shard_map(
        functools.partial(local, sizes),
        mesh=mesh,
        in_specs=(
            P(("dp", "ctx", "head"), None),
            P(("dp", "ctx"), "head"),
            P(("dp", "ctx"), "head"),
            P(("dp", "ctx", "head"), None),
            P(("dp", "ctx", "head"), None),
            P(("dp", "ctx", "head"), None),
            P("dp", None),
            P("dp"),
            P("dp"),
        ),
        out_specs=(
            P(("dp", "ctx", "head"), None),
            P(("dp", "ctx"), "head"),
            P(("dp", "ctx"), "head"),
        ),
        check_vma=False,
    )
```

```python
import functools
import math

import jax
import jax.numpy as jnp
from jax import lax
from jax.experimental import pallas as pl
from jax.experimental.pallas import tpu as pltpu
from jax.sharding import PartitionSpec as P

HEAD_DIM = 128
DISPATCH = 4
KCHUNK = 64
QCHUNK = 16
RING_X = 4
MESH = pl.DeviceIdType.MESH
F32 = jnp.float32
BF16 = jnp.bfloat16


def dot_nt(lhs, rhs):
    return lax.dot_general(lhs, rhs, (((1,), (1,)), ((), ())), preferred_element_type=F32)


def dot_nn(lhs, rhs):
    return lax.dot_general(lhs, rhs, (((1,), (0,)), ((), ())), preferred_element_type=F32)


def kernel(
    sizes,
    q_hbm,
    k_hbm,
    v_hbm,
    o_hbm,
    g_hbm,
    norm_hbm,
    table_hbm,
    key_order_hbm,
    query_order_hbm,
    dq_out,
    dk_out,
    dv_out,
    qg_all,
    nd_all,
    k_all,
    v_all,
    q_own,
    o_own,
    g_own,
    norm_own,
    nd_own,
    nd_rows,
    table,
    key_order,
    query_order,
    bias,
    dq_acc,
    dq_send,
    dq_recv,
    part_k,
    part_v,
    chain_send,
    chain_recv,
    dq_stage,
    dk_stage,
    dv_stage,
    load_sem,
    own_sem,
    relay_sem,
    qg_send_sem,
    nd_send_sem,
    qg_recv_sem,
    nd_recv_sem,
    ring_send,
    ring_recv,
    chain_send_sem,
    chain_recv_sem,
    dq_send_sem,
    dq_recv_sem,
    store_sem,
):
    size_z, size_x, size_y = sizes
    half = size_z // 2
    plane = size_x * size_y
    rows = plane * QCHUNK
    key_count = k_hbm.shape[0]
    heads_all = norm_hbm.shape[1]
    heads_loc = heads_all // size_y
    width = heads_loc * HEAD_DIM
    score_scale = 1.0 / math.sqrt(HEAD_DIM)
    log2e = math.log2(math.e)

    ctx = lax.axis_index("ctx")
    my_y = lax.axis_index("head")
    my_z = ctx // size_x
    my_x = ctx % size_x
    me = my_x * size_y + my_y
    my_rows = pl.ds(pl.multiple_of(me * QCHUNK, QCHUNK), QCHUNK)
    my_cols = pl.ds(pl.multiple_of(my_y * width, 128), width)

    def ring_z(offset):
        return (my_z + offset + size_z) % size_z

    def device(dz, dx, dy):
        return {
            "ctx": ring_z(dz) * size_x + (my_x + dx + size_x) % size_x,
            "head": (my_y + dy + size_y) % size_y,
        }

    def z_device(offset):
        return device(offset, 0, 0)

    def chunk_rows(sx, sy):
        chunk = (my_x + sx + size_x) % size_x * size_y + (my_y + sy + size_y) % size_y
        return pl.ds(pl.multiple_of(chunk * QCHUNK, QCHUNK), QCHUNK)

    own_k = k_all.at[my_z]
    own_v = v_all.at[my_z]
    loads = [
        pltpu.make_async_copy(k_hbm, own_k, load_sem.at[0]),
        pltpu.make_async_copy(v_hbm, own_v, load_sem.at[1]),
        pltpu.make_async_copy(g_hbm, g_own, load_sem.at[2]),
        pltpu.make_async_copy(o_hbm, o_own, load_sem.at[3]),
        pltpu.make_async_copy(norm_hbm, norm_own, load_sem.at[4]),
        pltpu.make_async_copy(q_hbm, q_own, load_sem.at[5]),
        pltpu.make_async_copy(table_hbm, table, load_sem.at[6]),
        pltpu.make_async_copy(key_order_hbm, key_order, load_sem.at[7]),
        pltpu.make_async_copy(query_order_hbm, query_order, load_sem.at[8]),
    ]
    for copy in loads:
        copy.start()

    barrier = pltpu.get_barrier_semaphore()
    neighbours = [(1, 0, 0), (-1, 0, 0), (0, 1, 0), (0, -1, 0), (0, 0, 1), (0, 0, -1)]
    for neighbour in neighbours:
        pl.semaphore_signal(
            barrier, inc=1, device_id=device(*neighbour), device_id_type=MESH
        )

    for copy in loads:
        copy.wait()

    lane = lax.broadcasted_iota(jnp.int32, (QCHUNK, 128), 1)
    tile = jnp.zeros((QCHUNK, 128), F32)
    for head in range(heads_all):
        cols = pl.ds(head * HEAD_DIM, HEAD_DIM)
        delta = jnp.sum(
            g_own[:, cols].astype(F32) * o_own[:, cols].astype(F32), axis=1, keepdims=True
        )
        tile = jnp.where(lane == heads_all + head, delta, tile)
    nd_own[...] = tile
    nd_own[:, 0:heads_all] = norm_own[...] * log2e

    pl.semaphore_wait(barrier, len(neighbours))

    for way in (1, -1):
        pl.semaphore_signal(
            relay_sem, inc=1, device_id=device(0, 0, way), device_id_type=MESH
        )

    def ring_copy(ref, way, step, index):
        slot = ring_z(-way * (step - 1))
        return pltpu.make_async_remote_copy(
            src_ref=ref.at[slot],
            dst_ref=ref.at[slot],
            send_sem=ring_send.at[index],
            recv_sem=ring_recv.at[index],
            device_id=z_device(way),
            device_id_type=MESH,
        )

    ring_plan = []
    for ref, way, steps in (
        (k_all, 1, half),
        (v_all, -1, half),
        (v_all, 1, half - 1),
        (k_all, -1, half - 1),
    ):
        ring_plan.append((ref, way, steps))
    ring = {}
    count = 0
    for step in range(1, half + 1):
        for line, (ref, way, steps) in enumerate(ring_plan):
            if step <= steps:
                ring[(line, step)] = ring_copy(ref, way, step, count)
                count += 1
    for line in range(4):
        if (line, 1) in ring:
            ring[(line, 1)].start()

    def slot_of(sx, sy):
        return (sx + 2 * size_x) % size_x * size_y + (sy + 2 * size_y) % size_y

    def plane_copy(src, dst, sends, receives, tx, ty, sx, sy):
        slot = slot_of(sx - tx, sy - ty)
        pltpu.make_async_remote_copy(
            src_ref=src,
            dst_ref=dst,
            send_sem=sends,
            recv_sem=receives.at[slot],
            device_id=device(0, tx, ty),
            device_id_type=MESH,
        ).start()

    def send_own(tx, ty):
        group = (my_y + ty + size_y) % size_y
        cols = pl.ds(pl.multiple_of(group * width, 128), width)
        for part, src in enumerate((q_own, g_own)):
            plane_copy(
                src.at[:, cols],
                qg_all.at[my_rows, pl.ds(part * width, width)],
                qg_send_sem,
                qg_recv_sem,
                tx,
                ty,
                0,
                0,
            )
        plane_copy(nd_own, nd_all.at[my_rows], nd_send_sem, nd_recv_sem, tx, ty, 0, 0)

    def wait_chunk(sx, sy):
        at = chunk_rows(sx, sy)
        slot = slot_of(sx, sy)
        pltpu.make_async_copy(qg_all.at[at], qg_all.at[at], qg_recv_sem.at[slot]).wait()
        pltpu.make_async_copy(nd_all.at[at], nd_all.at[at], nd_recv_sem.at[slot]).wait()

    def forward(sx, sy, way):
        at = chunk_rows(sx, sy)
        plane_copy(qg_all.at[at], qg_all.at[at], qg_send_sem, qg_recv_sem, way, 0, sx, sy)
        plane_copy(nd_all.at[at], nd_all.at[at], nd_send_sem, nd_recv_sem, way, 0, sx, sy)

    def ring_step(step):
        for line in range(4):
            if (line, step - 1) in ring:
                ring[(line, step - 1)].wait_recv()
            if (line, step) in ring:
                ring[(line, step)].start()

    send_own(0, 1)
    send_own(0, -1)
    send_own(1, 0)
    send_own(-1, 0)
    own_copies = [
        pltpu.make_async_copy(nd_own, nd_all.at[my_rows], own_sem.at[0]),
        pltpu.make_async_copy(
            q_own.at[:, my_cols], qg_all.at[my_rows, pl.ds(0, width)], own_sem.at[1]
        ),
        pltpu.make_async_copy(
            g_own.at[:, my_cols], qg_all.at[my_rows, pl.ds(width, width)], own_sem.at[2]
        ),
    ]
    for copy in own_copies:
        copy.start()
    pl.semaphore_wait(relay_sem, 2)
    send_own(0, 2)

    qlane = lax.broadcasted_iota(jnp.int32, (1, rows), 1)
    qpos = jnp.zeros((1, rows), jnp.int32)
    for chunk in range(plane):
        qpos = jnp.where(qlane // QCHUNK == chunk, query_order[my_z * plane + chunk], qpos)
    offset = key_order.shape[0] * KCHUNK - query_order.shape[0] * QCHUNK
    qpos = offset + qpos * QCHUNK + qlane % QCHUNK
    low = jnp.zeros((1, rows), jnp.int32)
    high = jnp.zeros((1, rows), jnp.int32)
    for row in range(table.shape[1]):
        inside = (qpos >= table[0, row]) & (qpos < table[1, row])
        last = jnp.where(table[4, row] != 0, jnp.minimum(table[3, row], qpos + 1), table[3, row])
        low = jnp.where(inside, table[2, row], low)
        high = jnp.where(inside, last, high)
    krow = lax.broadcasted_iota(jnp.int32, (KCHUNK, rows), 0)
    dq_acc[...] = jnp.zeros_like(dq_acc)

    for sy in (-1, 1):
        wait_chunk(0, sy)
        forward(0, sy, 1)
        forward(0, sy, -1)
    if half > 1:
        ring_step(2)
    wait_chunk(0, 2)
    forward(0, 2, 1)
    forward(0, 2, -1)
    for sy in (0, 1):
        wait_chunk(-1, sy)
        forward(-1, sy, 1)
    for sy in (-1, 2):
        wait_chunk(1, sy)
        forward(1, sy, -1)
    for step in range(3, half):
        ring_step(step)
    for sy in (0, 1):
        wait_chunk(1, sy)
    for sy in (-1, 2):
        wait_chunk(-1, sy)
    for sy in range(size_y):
        wait_chunk(2, sy)
    for copy in own_copies:
        copy.wait()
    turned = nd_all[...].T
    nd_rows[...] = turned[0 : 2 * heads_all]

    order = [0, half - 1, 1 - half, half]
    for distance in range(half - 2, 0, -1):
        order += [distance, -distance]

    def by_head(first):
        return jnp.concatenate(
            [qg_all[:, pl.ds(first + head * HEAD_DIM, HEAD_DIM)] for head in range(heads_loc)],
            axis=0,
        )

    def block_terms(index, dist):
        zb = ring_z(dist)
        first = (zb * size_x + my_x) * DISPATCH
        for part in range(DISPATCH):
            base = key_order[first + part] * KCHUNK
            ok = (krow >= low - base) & (krow < high - base)
            bias[pl.ds(part * KCHUNK, KCHUNK), :] = jnp.where(ok, jnp.inf, -jnp.inf).astype(F32)
        key_blk = k_all[zb]
        value_blk = v_all[zb]
        weights_low = []
        dscores = []
        for head in range(heads_loc):
            cols = pl.ds(head * HEAD_DIM, HEAD_DIM)
            norm = nd_rows[pl.ds(my_y * heads_loc + head, 1), :]
            delta = nd_rows[pl.ds(heads_all + my_y * heads_loc + head, 1), :]
            scores = dot_nt(key_blk, qg_all[:, cols])
            weights = jnp.exp2(jnp.minimum(scores * (score_scale * log2e) - norm, bias[...]))
            dprobs = dot_nt(value_blk, qg_all[:, pl.ds(width + head * HEAD_DIM, HEAD_DIM)])
            weights_low.append(weights.astype(BF16))
            dscores.append((weights * (dprobs - delta)).astype(BF16))
        part_v[index] = dot_nn(jnp.concatenate(weights_low, axis=1), by_head(width))
        part_k[index] = dot_nn(jnp.concatenate(dscores, axis=1), by_head(0))
        key_turned = key_blk.T
        for head in range(heads_loc):
            dq_acc[:, pl.ds(head * rows, rows)] += dot_nn(key_turned, dscores[head])

    slots = {}
    for dist in range(half - 1, 0, -1):
        for way in (1, -1):
            for kind in ("k", "v"):
                slots[(kind, way, dist)] = len(slots)
    far = {("k", 1): len(slots), ("v", -1): len(slots) + 1}

    def slot_copy(slot, dz):
        return pltpu.make_async_remote_copy(
            src_ref=chain_send.at[slot],
            dst_ref=chain_recv.at[slot],
            send_sem=chain_send_sem.at[slot],
            recv_sem=chain_recv_sem.at[slot],
            device_id=z_device(dz),
            device_id_type=MESH,
        )

    def chain_copy(kind, way, dist):
        return slot_copy(slots[(kind, way, dist)], way)

    def far_copy(kind, way):
        return slot_copy(far[(kind, way)], way * (half - 1))

    def chain_step(kind, way, dist):
        value = (part_k if kind == "k" else part_v)[order.index(way * dist)]
        if dist < half - 1:
            chain_copy(kind, way, dist + 1).wait_recv()
            value = value + chain_recv[slots[(kind, way, dist + 1)]].astype(F32)
        if dist == 1 and (kind, way) in far:
            far_copy(kind, way).wait_recv()
            value = value + chain_recv[far[(kind, way)]].astype(F32)
        chain_send[slots[(kind, way, dist)]] = value.astype(BF16)
        chain_copy(kind, way, dist).start()

    def far_step():
        for (kind, way), slot in far.items():
            value = (part_k if kind == "k" else part_v)[order.index(half)]
            chain_send[slot] = value.astype(BF16)
            far_copy(kind, way).start()

    def dist_at(index):
        later = index - 4
        near = half - 2 - later // 2
        return jnp.where(
            index == 0,
            0,
            jnp.where(
                index == 1,
                half - 1,
                jnp.where(
                    index == 2,
                    1 - half,
                    jnp.where(index == 3, half, jnp.where(later % 2 == 0, near, -near)),
                ),
            ),
        )

    def block_step(index, carry):
        @pl.when(index == 1)
        def _():
            ring_step(half)

        @pl.when(index == 3)
        def _():
            ring_step(half + 1)

        block_terms(index, dist_at(index))

        for at in range(1, size_z):
            dist = order[at]
            if dist == half or abs(dist) > 1:

                @pl.when(index == at)
                def _(dist=dist):
                    if dist == half:
                        far_step()
                    else:
                        way = 1 if dist > 0 else -1
                        chain_step("k", way, abs(dist))
                        chain_step("v", way, abs(dist))

        return carry

    lax.fori_loop(0, size_z, block_step, 0)

    peers = [(dx, dy) for dx in range(size_x) for dy in range(size_y) if dx or dy]
    peers.sort(key=lambda p: -(min(p[0], size_x - p[0]) + min(p[1], size_y - p[1])))
    for head in range(heads_loc):
        turned = dq_acc[:, pl.ds(head * rows, rows)].T
        dq_send[:, pl.ds(head * HEAD_DIM, HEAD_DIM)] = turned.astype(BF16)
    for dx, dy in peers:
        pltpu.make_async_remote_copy(
            src_ref=dq_send.at[chunk_rows(dx, dy)],
            dst_ref=dq_recv.at[my_x, :, my_cols],
            send_sem=dq_send_sem,
            recv_sem=dq_recv_sem,
            device_id=device(0, dx, dy),
            device_id_type=MESH,
        ).start()
    pltpu.make_async_copy(
        dq_send.at[my_rows], dq_recv.at[my_x, :, my_cols], dq_recv_sem
    ).start()

    for way in (1, -1):
        for kind in ("k", "v"):
            chain_step(kind, way, 1)

    pltpu.make_async_copy(dq_recv, dq_recv, dq_recv_sem).wait()
    total = dq_recv[0].astype(F32)
    for other in range(1, size_x):
        total = total + dq_recv[other].astype(F32)
    dq_stage[...] = (total * score_scale).astype(BF16)
    stores = [pltpu.make_async_copy(dq_stage, dq_out, store_sem.at[0])]
    stores[0].start()

    for kind, part, stage, out, scale in (
        ("v", part_v, dv_stage, dv_out, 1.0),
        ("k", part_k, dk_stage, dk_out, score_scale),
    ):
        value = part[0]
        for way in (1, -1):
            chain_copy(kind, way, 1).wait_recv()
            value = value + chain_recv[slots[(kind, way, 1)]].astype(F32)
        stage[...] = (value * scale).astype(BF16)
        stores.append(pltpu.make_async_copy(stage, out, store_sem.at[len(stores)]))
        stores[-1].start()

    for copy in ring.values():
        copy.wait_send()
    for key in slots:
        chain_copy(*key).wait_send()
    for key in far:
        far_copy(*key).wait_send()
    sent = pl.ds(0, len(peers) * QCHUNK)
    pltpu.make_async_copy(qg_all.at[sent], qg_all.at[sent], qg_send_sem).wait()
    pltpu.make_async_copy(nd_all.at[sent], nd_all.at[sent], nd_send_sem).wait()
    pltpu.make_async_copy(dq_send.at[sent], dq_send.at[sent], dq_send_sem).wait()
    for copy in stores:
        copy.wait()


def local(
    sizes,
    query_rows,
    key_rows,
    value_rows,
    output_rows,
    grad_out,
    log_norm,
    mask_table,
    key_order,
    query_order,
):
    size_z, size_x, size_y = sizes
    half = size_z // 2
    rows = size_x * size_y * QCHUNK
    key_count = key_rows.shape[0]
    own, columns = query_rows.shape
    heads_all = log_norm.shape[1]
    width = columns // size_y
    chain = 2 * (2 * half - 1)
    hbm = pl.BlockSpec(memory_space=pltpu.HBM)
    dma = pltpu.SemaphoreType.DMA
    return pl.pallas_call(
        functools.partial(kernel, sizes),
        out_shape=(
            jax.ShapeDtypeStruct(query_rows.shape, BF16),
            jax.ShapeDtypeStruct(key_rows.shape, BF16),
            jax.ShapeDtypeStruct(value_rows.shape, BF16),
        ),
        in_specs=[hbm] * 9,
        out_specs=(hbm, hbm, hbm),
        scratch_shapes=[
            pltpu.VMEM((rows, 2 * width), BF16),
            pltpu.VMEM((rows, 128), F32),
            pltpu.VMEM((size_z, key_count, HEAD_DIM), BF16),
            pltpu.VMEM((size_z, key_count, HEAD_DIM), BF16),
            pltpu.VMEM((own, columns), BF16),
            pltpu.VMEM((own, columns), BF16),
            pltpu.VMEM((own, columns), BF16),
            pltpu.VMEM((own, heads_all), F32),
            pltpu.VMEM((own, 128), F32),
            pltpu.VMEM((2 * heads_all, rows), F32),
            pltpu.SMEM(mask_table.shape[::-1], jnp.int32),
            pltpu.SMEM(key_order.shape, jnp.int32),
            pltpu.SMEM(query_order.shape, jnp.int32),
            pltpu.VMEM((key_count, rows), F32),
            pltpu.VMEM((HEAD_DIM, width // HEAD_DIM * rows), F32),
            pltpu.VMEM((rows, width), BF16),
            pltpu.VMEM((size_x, own, columns), BF16),
            pltpu.VMEM((size_z, key_count, HEAD_DIM), F32),
            pltpu.VMEM((size_z, key_count, HEAD_DIM), F32),
            pltpu.VMEM((chain, key_count, HEAD_DIM), BF16),
            pltpu.VMEM((chain, key_count, HEAD_DIM), BF16),
            pltpu.VMEM((own, columns), BF16),
            pltpu.VMEM((key_count, HEAD_DIM), BF16),
            pltpu.VMEM((key_count, HEAD_DIM), BF16),
            dma((9,)),
            dma((3,)),
            pltpu.SemaphoreType.REGULAR,
            dma,
            dma,
            dma((size_x * size_y,)),
            dma((size_x * size_y,)),
            dma((chain,)),
            dma((chain,)),
            dma((chain,)),
            dma((chain,)),
            dma,
            dma,
            dma((3,)),
        ],
        compiler_params=pltpu.CompilerParams(
            collective_id=0, has_side_effects=True, vmem_limit_bytes=60 * 1024 * 1024
        ),
    )(
        query_rows,
        key_rows,
        value_rows,
        output_rows,
        grad_out,
        log_norm,
        mask_table.T,
        key_order,
        query_order,
    )


def solution(mesh, ring_x=RING_X):
    sizes = (mesh.shape["ctx"] // ring_x, ring_x, mesh.shape["head"])
    return jax.shard_map(
        functools.partial(local, sizes),
        mesh=mesh,
        in_specs=(
            P(("dp", "ctx", "head"), None),
            P(("dp", "ctx"), "head"),
            P(("dp", "ctx"), "head"),
            P(("dp", "ctx", "head"), None),
            P(("dp", "ctx", "head"), None),
            P(("dp", "ctx", "head"), None),
            P("dp", None),
            P("dp"),
            P("dp"),
        ),
        out_specs=(
            P(("dp", "ctx", "head"), None),
            P(("dp", "ctx"), "head"),
            P(("dp", "ctx"), "head"),
        ),
        check_vma=False,
    )
```

```python
import functools
import math

import jax
import jax.numpy as jnp
from jax import lax
from jax.experimental import pallas as pl
from jax.experimental.pallas import tpu as pltpu
from jax.sharding import PartitionSpec as P

HEAD_DIM = 128
DISPATCH = 4
KCHUNK = 64
QCHUNK = 16
RING_X = 4
MESH = pl.DeviceIdType.MESH
F32 = jnp.float32
BF16 = jnp.bfloat16


def dot_nt(lhs, rhs):
    return lax.dot_general(lhs, rhs, (((1,), (1,)), ((), ())), preferred_element_type=F32)


def dot_nn(lhs, rhs):
    return lax.dot_general(lhs, rhs, (((1,), (0,)), ((), ())), preferred_element_type=F32)


def kernel(
    sizes,
    q_hbm,
    k_hbm,
    v_hbm,
    o_hbm,
    g_hbm,
    norm_hbm,
    table_hbm,
    key_order_hbm,
    query_order_hbm,
    dq_recv,
    own_k,
    own_v,
    recv_k,
    recv_v,
    qg_all,
    nd_all,
    k_all,
    v_all,
    q_own,
    o_own,
    g_own,
    norm_own,
    nd_own,
    nd_rows,
    table,
    key_order,
    query_order,
    bias,
    dq_acc,
    dq_send,
    part_k,
    part_v,
    chain_send,
    chain_recv,
    load_sem,
    own_sem,
    relay_sem,
    qg_send_sem,
    nd_send_sem,
    qg_recv_sem,
    nd_recv_sem,
    ring_send,
    ring_recv,
    chain_send_sem,
    chain_recv_sem,
    dq_send_sem,
    dq_recv_sem,
    store_sem,
):
    size_z, size_x, size_y = sizes
    half = size_z // 2
    plane = size_x * size_y
    rows = plane * QCHUNK
    key_count = k_hbm.shape[0]
    heads_all = norm_hbm.shape[1]
    heads_loc = heads_all // size_y
    width = heads_loc * HEAD_DIM
    score_scale = 1.0 / math.sqrt(HEAD_DIM)
    log2e = math.log2(math.e)

    ctx = lax.axis_index("ctx")
    my_y = lax.axis_index("head")
    my_z = ctx // size_x
    my_x = ctx % size_x
    me = my_x * size_y + my_y
    my_rows = pl.ds(pl.multiple_of(me * QCHUNK, QCHUNK), QCHUNK)
    my_cols = pl.ds(pl.multiple_of(my_y * width, 128), width)

    def ring_z(offset):
        return (my_z + offset + size_z) % size_z

    def device(dz, dx, dy):
        return {
            "ctx": ring_z(dz) * size_x + (my_x + dx + size_x) % size_x,
            "head": (my_y + dy + size_y) % size_y,
        }

    def z_device(offset):
        return device(offset, 0, 0)

    def chunk_rows(sx, sy):
        chunk = (my_x + sx + size_x) % size_x * size_y + (my_y + sy + size_y) % size_y
        return pl.ds(pl.multiple_of(chunk * QCHUNK, QCHUNK), QCHUNK)

    barrier = pltpu.get_barrier_semaphore()
    neighbours = [(1, 0, 0), (-1, 0, 0), (0, 1, 0), (0, -1, 0), (0, 0, 1), (0, 0, -1)]
    for neighbour in neighbours:
        pl.semaphore_signal(
            barrier, inc=1, device_id=device(*neighbour), device_id_type=MESH
        )

    loads = [
        pltpu.make_async_copy(k_hbm, k_all.at[my_z], load_sem.at[0]),
        pltpu.make_async_copy(v_hbm, v_all.at[my_z], load_sem.at[1]),
        pltpu.make_async_copy(g_hbm, g_own, load_sem.at[2]),
        pltpu.make_async_copy(o_hbm, o_own, load_sem.at[3]),
        pltpu.make_async_copy(norm_hbm, norm_own, load_sem.at[4]),
        pltpu.make_async_copy(q_hbm, q_own, load_sem.at[5]),
        pltpu.make_async_copy(table_hbm, table, load_sem.at[6]),
        pltpu.make_async_copy(key_order_hbm, key_order, load_sem.at[7]),
        pltpu.make_async_copy(query_order_hbm, query_order, load_sem.at[8]),
    ]
    for copy in loads:
        copy.start()

    pl.semaphore_wait(barrier, len(neighbours))

    def ring_copy(ref, way, step, index):
        slot = ring_z(-way * (step - 1))
        src = ref.at[slot] if step > 1 else (k_hbm if ref is k_all else v_hbm)
        return pltpu.make_async_remote_copy(
            src_ref=src,
            dst_ref=ref.at[slot],
            send_sem=ring_send.at[index],
            recv_sem=ring_recv.at[index],
            device_id=z_device(way),
            device_id_type=MESH,
        )

    ring_plan = []
    for ref, way, steps in (
        (k_all, 1, half),
        (v_all, -1, half),
        (v_all, 1, half - 1),
        (k_all, -1, half - 1),
    ):
        ring_plan.append((ref, way, steps))
    ring = {}
    count = 0
    for step in range(1, half + 1):
        for line, (ref, way, steps) in enumerate(ring_plan):
            if step <= steps:
                ring[(line, step)] = ring_copy(ref, way, step, count)
                count += 1
    for line in range(4):
        if (line, 1) in ring:
            ring[(line, 1)].start()

    for way in (1, -1):
        pl.semaphore_signal(
            relay_sem, inc=1, device_id=device(0, 0, way), device_id_type=MESH
        )

    for copy in loads:
        copy.wait()

    lane = lax.broadcasted_iota(jnp.int32, (QCHUNK, 128), 1)
    tile = jnp.zeros((QCHUNK, 128), F32)
    for head in range(heads_all):
        cols = pl.ds(head * HEAD_DIM, HEAD_DIM)
        delta = jnp.sum(
            g_own[:, cols].astype(F32) * o_own[:, cols].astype(F32), axis=1, keepdims=True
        )
        tile = jnp.where(lane == heads_all + head, delta, tile)
    nd_own[...] = tile
    nd_own[:, 0:heads_all] = norm_own[...] * log2e

    def slot_of(sx, sy):
        return (sx + 2 * size_x) % size_x * size_y + (sy + 2 * size_y) % size_y

    def plane_copy(src, dst, sends, receives, tx, ty, sx, sy):
        slot = slot_of(sx - tx, sy - ty)
        pltpu.make_async_remote_copy(
            src_ref=src,
            dst_ref=dst,
            send_sem=sends,
            recv_sem=receives.at[slot],
            device_id=device(0, tx, ty),
            device_id_type=MESH,
        ).start()

    def send_own(tx, ty):
        group = (my_y + ty + size_y) % size_y
        cols = pl.ds(pl.multiple_of(group * width, 128), width)
        for part, src in enumerate((q_own, g_own)):
            plane_copy(
                src.at[:, cols],
                qg_all.at[my_rows, pl.ds(part * width, width)],
                qg_send_sem,
                qg_recv_sem,
                tx,
                ty,
                0,
                0,
            )
        plane_copy(nd_own, nd_all.at[my_rows], nd_send_sem, nd_recv_sem, tx, ty, 0, 0)

    def wait_chunk(sx, sy):
        at = chunk_rows(sx, sy)
        slot = slot_of(sx, sy)
        pltpu.make_async_copy(qg_all.at[at], qg_all.at[at], qg_recv_sem.at[slot]).wait()
        pltpu.make_async_copy(nd_all.at[at], nd_all.at[at], nd_recv_sem.at[slot]).wait()

    def forward(sx, sy, way):
        at = chunk_rows(sx, sy)
        plane_copy(qg_all.at[at], qg_all.at[at], qg_send_sem, qg_recv_sem, way, 0, sx, sy)
        plane_copy(nd_all.at[at], nd_all.at[at], nd_send_sem, nd_recv_sem, way, 0, sx, sy)

    def ring_step(step):
        for line in range(4):
            if (line, step - 1) in ring:
                ring[(line, step - 1)].wait_recv()
            if (line, step) in ring:
                ring[(line, step)].start()

    send_own(0, 1)
    send_own(0, -1)
    send_own(1, 0)
    send_own(-1, 0)
    own_copies = [
        pltpu.make_async_copy(nd_own, nd_all.at[my_rows], own_sem.at[0]),
        pltpu.make_async_copy(
            q_own.at[:, my_cols], qg_all.at[my_rows, pl.ds(0, width)], own_sem.at[1]
        ),
        pltpu.make_async_copy(
            g_own.at[:, my_cols], qg_all.at[my_rows, pl.ds(width, width)], own_sem.at[2]
        ),
    ]
    for copy in own_copies:
        copy.start()
    pl.semaphore_wait(relay_sem, 2)
    send_own(0, 2)

    qlane = lax.broadcasted_iota(jnp.int32, (1, rows), 1)
    qpos = jnp.zeros((1, rows), jnp.int32)
    for chunk in range(plane):
        qpos = jnp.where(qlane // QCHUNK == chunk, query_order[my_z * plane + chunk], qpos)
    offset = key_order.shape[0] * KCHUNK - query_order.shape[0] * QCHUNK
    qpos = offset + qpos * QCHUNK + qlane % QCHUNK
    low = jnp.zeros((1, rows), jnp.int32)
    high = jnp.zeros((1, rows), jnp.int32)
    for row in range(table.shape[1]):
        inside = (qpos >= table[0, row]) & (qpos < table[1, row])
        last = jnp.where(table[4, row] != 0, jnp.minimum(table[3, row], qpos + 1), table[3, row])
        low = jnp.where(inside, table[2, row], low)
        high = jnp.where(inside, last, high)
    krow = lax.broadcasted_iota(jnp.int32, (KCHUNK, rows), 0)
    dq_acc[...] = jnp.zeros_like(dq_acc)

    ring_step(2)
    for sy in (-1, 1):
        wait_chunk(0, sy)
        forward(0, sy, 1)
        forward(0, sy, -1)
    wait_chunk(0, 2)
    forward(0, 2, 1)
    forward(0, 2, -1)
    if half > 2:
        ring_step(3)
    for sy in (0, 1):
        wait_chunk(-1, sy)
        forward(-1, sy, 1)
    for sy in (-1, 2):
        wait_chunk(1, sy)
        forward(1, sy, -1)
    for step in range(4, half + 1):
        ring_step(step)
    for sy in (0, 1):
        wait_chunk(1, sy)
    for sy in (-1, 2):
        wait_chunk(-1, sy)
    for sy in range(size_y):
        wait_chunk(2, sy)
    for copy in own_copies:
        copy.wait()
    turned = nd_all[...].T
    nd_rows[...] = turned[0 : 2 * heads_all]

    order = [0, half]
    for distance in range(half - 1, 0, -1):
        order += [distance, -distance]

    def by_head(first):
        return jnp.concatenate(
            [qg_all[:, pl.ds(first + head * HEAD_DIM, HEAD_DIM)] for head in range(heads_loc)],
            axis=0,
        )

    def block_terms(index, dist):
        zb = ring_z(dist)
        first = (zb * size_x + my_x) * DISPATCH
        for part in range(DISPATCH):
            base = key_order[first + part] * KCHUNK
            ok = (krow >= low - base) & (krow < high - base)
            bias[pl.ds(part * KCHUNK, KCHUNK), :] = jnp.where(ok, jnp.inf, -jnp.inf).astype(F32)
        key_blk = k_all[zb]
        value_blk = v_all[zb]
        weights_low = []
        dscores = []
        for head in range(heads_loc):
            cols = pl.ds(head * HEAD_DIM, HEAD_DIM)
            norm = nd_rows[pl.ds(my_y * heads_loc + head, 1), :]
            delta = nd_rows[pl.ds(heads_all + my_y * heads_loc + head, 1), :]
            scores = dot_nt(key_blk, qg_all[:, cols])
            weights = jnp.exp2(jnp.minimum(scores * (score_scale * log2e) - norm, bias[...]))
            dprobs = dot_nt(value_blk, qg_all[:, pl.ds(width + head * HEAD_DIM, HEAD_DIM)])
            weights_low.append(weights.astype(BF16))
            dscores.append((weights * (dprobs - delta)).astype(BF16))
        part_v[index] = dot_nn(jnp.concatenate(weights_low, axis=1), by_head(width))
        part_k[index] = dot_nn(jnp.concatenate(dscores, axis=1), by_head(0))
        key_turned = key_blk.T
        for head in range(heads_loc):
            dq_acc[:, pl.ds(head * rows, rows)] += dot_nn(key_turned, dscores[head])

    lines = {("k", 1): half, ("v", -1): half, ("v", 1): half - 1, ("k", -1): half - 1}
    slots = {}
    for (kind, way), first_dist in lines.items():
        for dist in range(first_dist, 0, -1):
            slots[(kind, way, dist)] = len(slots)

    def chain_copy(kind, way, dist):
        slot = slots[(kind, way, dist)]
        dst = chain_recv.at[slot]
        if dist == 1:
            dst = (recv_k if kind == "k" else recv_v).at[0 if way == 1 else 1]
        return pltpu.make_async_remote_copy(
            src_ref=chain_send.at[slot],
            dst_ref=dst,
            send_sem=chain_send_sem.at[slot],
            recv_sem=chain_recv_sem.at[slot],
            device_id=z_device(way),
            device_id_type=MESH,
        )

    def chain_step(kind, way, dist):
        index = order.index(half if dist == half else way * dist)
        value = (part_k if kind == "k" else part_v)[index]
        if dist < lines[(kind, way)]:
            chain_copy(kind, way, dist + 1).wait_recv()
            value = value + chain_recv[slots[(kind, way, dist + 1)]].astype(F32)
        chain_send[slots[(kind, way, dist)]] = value.astype(BF16)
        chain_copy(kind, way, dist).start()

    events = {at: [] for at in range(size_z + 1)}
    for (kind, way), first_dist in lines.items():
        for dist in range(first_dist, 0, -1):
            at = order.index(half if dist == half else way * dist)
            if first_dist == half and dist < half:
                at = 4 + 3 * (half - 1 - dist)
            elif dist < half - 1:
                at = 5 + 3 * (half - 2 - dist) + (way < 0)
            events[min(at, size_z) if dist > 1 else size_z].append((kind, way, dist))
    for listed in events.values():
        listed.sort(key=lambda e: lines[(e[0], e[1])] - half)

    def dist_at(index):
        near = half - index // 2
        paired = jnp.where(index % 2 == 0, near, -near)
        return jnp.where(index == 0, 0, jnp.where(index == 1, half, paired))

    def block_step(index, carry):
        @pl.when(index == 1)
        def _():
            ring_step(half + 1)

        block_terms(index, dist_at(index))

        for at in range(1, size_z):
            if events[at]:

                @pl.when(index == at)
                def _(at=at):
                    for event in events[at]:
                        chain_step(*event)

        return carry

    lax.fori_loop(0, size_z, block_step, 0)

    stores = [
        pltpu.make_async_copy(part_k.at[0], own_k, store_sem.at[0]),
        pltpu.make_async_copy(part_v.at[0], own_v, store_sem.at[1]),
    ]
    for copy in stores:
        copy.start()

    peers = [(dx, dy) for dx in range(size_x) for dy in range(size_y) if dx or dy]
    peers.sort(key=lambda p: -(min(p[0], size_x - p[0]) + min(p[1], size_y - p[1])))
    for head in range(heads_loc):
        turned = dq_acc[:, pl.ds(head * rows, rows)].T
        dq_send[:, pl.ds(head * HEAD_DIM, HEAD_DIM)] = turned.astype(BF16)
    for dx, dy in peers:
        pltpu.make_async_remote_copy(
            src_ref=dq_send.at[chunk_rows(dx, dy)],
            dst_ref=dq_recv.at[my_x, :, my_cols],
            send_sem=dq_send_sem,
            recv_sem=dq_recv_sem,
            device_id=device(0, dx, dy),
            device_id_type=MESH,
        ).start()
    pltpu.make_async_copy(
        dq_send.at[my_rows], dq_recv.at[my_x, :, my_cols], dq_recv_sem
    ).start()

    for event in events[size_z]:
        chain_step(*event)

    pltpu.make_async_copy(dq_recv, dq_recv, dq_recv_sem).wait()
    for key in slots:
        if key[2] == 1:
            chain_copy(*key).wait_recv()

    for copy in ring.values():
        copy.wait_send()
    for key in slots:
        chain_copy(*key).wait_send()
    sent = pl.ds(0, len(peers) * QCHUNK)
    pltpu.make_async_copy(qg_all.at[sent], qg_all.at[sent], qg_send_sem).wait()
    pltpu.make_async_copy(nd_all.at[sent], nd_all.at[sent], nd_send_sem).wait()
    pltpu.make_async_copy(dq_send.at[sent], dq_send.at[sent], dq_send_sem).wait()
    for copy in stores:
        copy.wait()


def add_up_kernel(dq_recv, own_k, own_v, recv_k, recv_v, dq_out, dk_out, dv_out):
    score_scale = 1.0 / math.sqrt(HEAD_DIM)
    total = dq_recv[0].astype(F32)
    for other in range(1, dq_recv.shape[0]):
        total = total + dq_recv[other].astype(F32)
    dq_out[...] = (total * score_scale).astype(BF16)
    total = own_k[...] + recv_k[0].astype(F32) + recv_k[1].astype(F32)
    dk_out[...] = (total * score_scale).astype(BF16)
    total = own_v[...] + recv_v[0].astype(F32) + recv_v[1].astype(F32)
    dv_out[...] = total.astype(BF16)


def add_up(terms):
    vmem = pl.BlockSpec(memory_space=pltpu.VMEM)
    dq_recv, own_k, own_v = terms[:3]
    return pl.pallas_call(
        add_up_kernel,
        out_shape=(
            jax.ShapeDtypeStruct(dq_recv.shape[1:], BF16),
            jax.ShapeDtypeStruct(own_k.shape, BF16),
            jax.ShapeDtypeStruct(own_v.shape, BF16),
        ),
        in_specs=[vmem] * 5,
        out_specs=(vmem,) * 3,
        name="add_up",
        compiler_params=pltpu.CompilerParams(vmem_limit_bytes=60 * 1024 * 1024),
    )(*terms)


def local(
    sizes,
    query_rows,
    key_rows,
    value_rows,
    output_rows,
    grad_out,
    log_norm,
    mask_table,
    key_order,
    query_order,
):
    size_z, size_x, size_y = sizes
    half = size_z // 2
    rows = size_x * size_y * QCHUNK
    key_count = key_rows.shape[0]
    own, columns = query_rows.shape
    heads_all = log_norm.shape[1]
    width = columns // size_y
    chain = 2 * (2 * half - 1)
    hbm = pl.BlockSpec(memory_space=pltpu.HBM)
    dma = pltpu.SemaphoreType.DMA
    terms = pl.pallas_call(
        functools.partial(kernel, sizes),
        out_shape=(
            jax.ShapeDtypeStruct((size_x,) + query_rows.shape, BF16),
            jax.ShapeDtypeStruct(key_rows.shape, F32),
            jax.ShapeDtypeStruct(value_rows.shape, F32),
            jax.ShapeDtypeStruct((2,) + key_rows.shape, BF16),
            jax.ShapeDtypeStruct((2,) + value_rows.shape, BF16),
        ),
        in_specs=[hbm] * 9,
        out_specs=(hbm,) * 5,
        scratch_shapes=[
            pltpu.VMEM((rows, 2 * width), BF16),
            pltpu.VMEM((rows, 128), F32),
            pltpu.VMEM((size_z, key_count, HEAD_DIM), BF16),
            pltpu.VMEM((size_z, key_count, HEAD_DIM), BF16),
            pltpu.VMEM((own, columns), BF16),
            pltpu.VMEM((own, columns), BF16),
            pltpu.VMEM((own, columns), BF16),
            pltpu.VMEM((own, heads_all), F32),
            pltpu.VMEM((own, 128), F32),
            pltpu.VMEM((2 * heads_all, rows), F32),
            pltpu.SMEM(mask_table.shape[::-1], jnp.int32),
            pltpu.SMEM(key_order.shape, jnp.int32),
            pltpu.SMEM(query_order.shape, jnp.int32),
            pltpu.VMEM((key_count, rows), F32),
            pltpu.VMEM((HEAD_DIM, width // HEAD_DIM * rows), F32),
            pltpu.VMEM((rows, width), BF16),
            pltpu.VMEM((size_z, key_count, HEAD_DIM), F32),
            pltpu.VMEM((size_z, key_count, HEAD_DIM), F32),
            pltpu.VMEM((chain, key_count, HEAD_DIM), BF16),
            pltpu.VMEM((chain, key_count, HEAD_DIM), BF16),
            dma((9,)),
            dma((3,)),
            pltpu.SemaphoreType.REGULAR,
            dma,
            dma,
            dma((size_x * size_y,)),
            dma((size_x * size_y,)),
            dma((chain,)),
            dma((chain,)),
            dma((chain,)),
            dma((chain,)),
            dma,
            dma,
            dma((2,)),
        ],
        compiler_params=pltpu.CompilerParams(
            collective_id=0, has_side_effects=True, vmem_limit_bytes=60 * 1024 * 1024
        ),
    )(
        query_rows,
        key_rows,
        value_rows,
        output_rows,
        grad_out,
        log_norm,
        mask_table.T,
        key_order,
        query_order,
    )
    return add_up(terms)


def solution(mesh, ring_x=RING_X):
    sizes = (mesh.shape["ctx"] // ring_x, ring_x, mesh.shape["head"])
    return jax.shard_map(
        functools.partial(local, sizes),
        mesh=mesh,
        in_specs=(
            P(("dp", "ctx", "head"), None),
            P(("dp", "ctx"), "head"),
            P(("dp", "ctx"), "head"),
            P(("dp", "ctx", "head"), None),
            P(("dp", "ctx", "head"), None),
            P(("dp", "ctx", "head"), None),
            P("dp", None),
            P("dp"),
            P("dp"),
        ),
        out_specs=(
            P(("dp", "ctx", "head"), None),
            P(("dp", "ctx"), "head"),
            P(("dp", "ctx"), "head"),
        ),
        check_vma=False,
    )
```

```python
import functools
import math

import jax
import jax.numpy as jnp
from jax import lax
from jax.experimental import pallas as pl
from jax.experimental.pallas import tpu as pltpu
from jax.sharding import PartitionSpec as P

HEAD_DIM = 128
DISPATCH = 4
KCHUNK = 64
QCHUNK = 16
RING_X = 4
MESH = pl.DeviceIdType.MESH
F32 = jnp.float32
BF16 = jnp.bfloat16


def dot_nt(lhs, rhs):
    return lax.dot_general(lhs, rhs, (((1,), (1,)), ((), ())), preferred_element_type=F32)


def dot_nn(lhs, rhs):
    return lax.dot_general(lhs, rhs, (((1,), (0,)), ((), ())), preferred_element_type=F32)


def kernel(
    sizes,
    q_hbm,
    k_hbm,
    v_hbm,
    o_hbm,
    g_hbm,
    norm_hbm,
    table_hbm,
    key_order_hbm,
    query_order_hbm,
    dq_recv,
    own_k,
    own_v,
    recv_k,
    recv_v,
    qg_all,
    nd_all,
    k_all,
    v_all,
    o_own,
    g_own,
    norm_own,
    nd_own,
    nd_rows,
    table,
    key_order,
    query_order,
    bias,
    dq_acc,
    dq_send,
    part_k,
    part_v,
    chain_send,
    chain_recv,
    load_sem,
    own_sem,
    relay_sem,
    relay_x_sem,
    qg_send_sem,
    nd_send_sem,
    qg_recv_sem,
    nd_recv_sem,
    ring_send,
    ring_recv,
    chain_send_sem,
    chain_recv_sem,
    dq_send_sem,
    dq_recv_sem,
    store_sem,
):
    size_z, size_x, size_y = sizes
    half = size_z // 2
    plane = size_x * size_y
    rows = plane * QCHUNK
    key_count = k_hbm.shape[0]
    heads_all = norm_hbm.shape[1]
    heads_loc = heads_all // size_y
    width = heads_loc * HEAD_DIM
    score_scale = 1.0 / math.sqrt(HEAD_DIM)
    log2e = math.log2(math.e)

    ctx = lax.axis_index("ctx")
    my_y = lax.axis_index("head")
    my_z = ctx // size_x
    my_x = ctx % size_x
    me = my_x * size_y + my_y
    my_rows = pl.ds(pl.multiple_of(me * QCHUNK, QCHUNK), QCHUNK)
    my_cols = pl.ds(pl.multiple_of(my_y * width, 128), width)

    def ring_z(offset):
        return (my_z + offset + size_z) % size_z

    def device(dz, dx, dy):
        return {
            "ctx": ring_z(dz) * size_x + (my_x + dx + size_x) % size_x,
            "head": (my_y + dy + size_y) % size_y,
        }

    def z_device(offset):
        return device(offset, 0, 0)

    def chunk_rows(sx, sy):
        chunk = (my_x + sx + size_x) % size_x * size_y + (my_y + sy + size_y) % size_y
        return pl.ds(pl.multiple_of(chunk * QCHUNK, QCHUNK), QCHUNK)

    barrier = pltpu.get_barrier_semaphore()
    neighbours = [(1, 0, 0), (-1, 0, 0), (0, 1, 0), (0, -1, 0), (0, 0, 1), (0, 0, -1)]
    for neighbour in neighbours:
        pl.semaphore_signal(
            barrier, inc=1, device_id=device(*neighbour), device_id_type=MESH
        )

    pl.semaphore_wait(barrier, len(neighbours))

    def ring_copy(ref, way, step, index):
        slot = ring_z(-way * (step - 1))
        src = ref.at[slot] if step > 1 else (k_hbm if ref is k_all else v_hbm)
        return pltpu.make_async_remote_copy(
            src_ref=src,
            dst_ref=ref.at[slot],
            send_sem=ring_send.at[index],
            recv_sem=ring_recv.at[index],
            device_id=z_device(way),
            device_id_type=MESH,
        )

    ring_plan = []
    for ref, way, steps in (
        (k_all, 1, half),
        (v_all, -1, half),
        (v_all, 1, half - 1),
        (k_all, -1, half - 1),
    ):
        ring_plan.append((ref, way, steps))
    ring = {}
    count = 0
    for step in range(1, half + 1):
        for line, (ref, way, steps) in enumerate(ring_plan):
            if step <= steps:
                ring[(line, step)] = ring_copy(ref, way, step, count)
                count += 1
    for line in range(4):
        if (line, 1) in ring:
            ring[(line, 1)].start()

    for way in (1, -1):
        pl.semaphore_signal(
            relay_sem, inc=1, device_id=device(0, 0, way), device_id_type=MESH
        )

    loads = [
        pltpu.make_async_copy(k_hbm, k_all.at[my_z], load_sem.at[0]),
        pltpu.make_async_copy(v_hbm, v_all.at[my_z], load_sem.at[1]),
        pltpu.make_async_copy(g_hbm, g_own, load_sem.at[2]),
        pltpu.make_async_copy(o_hbm, o_own, load_sem.at[3]),
        pltpu.make_async_copy(norm_hbm, norm_own, load_sem.at[4]),
        pltpu.make_async_copy(table_hbm, table, load_sem.at[5]),
        pltpu.make_async_copy(key_order_hbm, key_order, load_sem.at[6]),
        pltpu.make_async_copy(query_order_hbm, query_order, load_sem.at[7]),
    ]
    for copy in loads:
        copy.start()

    def slot_of(sx, sy):
        return (sx + 2 * size_x) % size_x * size_y + (sy + 2 * size_y) % size_y

    def plane_copy(src, dst, sends, receives, tx, ty, sx, sy):
        slot = slot_of(sx - tx, sy - ty)
        pltpu.make_async_remote_copy(
            src_ref=src,
            dst_ref=dst,
            send_sem=sends,
            recv_sem=receives.at[slot],
            device_id=device(0, tx, ty),
            device_id_type=MESH,
        ).start()

    def send_rows(tx, ty):
        group = (my_y + ty + size_y) % size_y
        cols = pl.ds(pl.multiple_of(group * width, 128), width)
        for part, src in enumerate((q_hbm, g_hbm)):
            plane_copy(
                src.at[:, cols],
                qg_all.at[my_rows, pl.ds(part * width, width)],
                qg_send_sem,
                qg_recv_sem,
                tx,
                ty,
                0,
                0,
            )

    def send_nd(tx, ty):
        plane_copy(nd_own, nd_all.at[my_rows], nd_send_sem, nd_recv_sem, tx, ty, 0, 0)

    def wait_chunk(sx, sy):
        at = chunk_rows(sx, sy)
        slot = slot_of(sx, sy)
        pltpu.make_async_copy(qg_all.at[at], qg_all.at[at], qg_recv_sem.at[slot]).wait()
        pltpu.make_async_copy(nd_all.at[at], nd_all.at[at], nd_recv_sem.at[slot]).wait()

    def forward(sx, sy, way):
        at = chunk_rows(sx, sy)
        plane_copy(qg_all.at[at], qg_all.at[at], qg_send_sem, qg_recv_sem, way, 0, sx, sy)
        plane_copy(nd_all.at[at], nd_all.at[at], nd_send_sem, nd_recv_sem, way, 0, sx, sy)

    def ring_step(step):
        for line in range(4):
            if (line, step - 1) in ring:
                ring[(line, step - 1)].wait_recv()
            if (line, step) in ring:
                ring[(line, step)].start()

    beside = ((0, 1), (0, -1), (1, 0), (-1, 0))
    for peer in beside:
        send_rows(*peer)
    own_copies = [
        pltpu.make_async_copy(
            q_hbm.at[:, my_cols], qg_all.at[my_rows, pl.ds(0, width)], own_sem.at[1]
        ),
        pltpu.make_async_copy(
            g_hbm.at[:, my_cols], qg_all.at[my_rows, pl.ds(width, width)], own_sem.at[2]
        ),
    ]
    for copy in own_copies:
        copy.start()

    for copy in loads:
        copy.wait()

    lane = lax.broadcasted_iota(jnp.int32, (QCHUNK, 128), 1)
    tile = jnp.zeros((QCHUNK, 128), F32)
    for head in range(heads_all):
        cols = pl.ds(head * HEAD_DIM, HEAD_DIM)
        delta = jnp.sum(
            g_own[:, cols].astype(F32) * o_own[:, cols].astype(F32), axis=1, keepdims=True
        )
        tile = jnp.where(lane == heads_all + head, delta, tile)
    nd_own[...] = tile
    nd_own[:, 0:heads_all] = norm_own[...] * log2e

    for peer in beside:
        send_nd(*peer)
    own_copies.append(pltpu.make_async_copy(nd_own, nd_all.at[my_rows], own_sem.at[0]))
    own_copies[-1].start()
    pl.semaphore_wait(relay_sem, 2)
    for way in (1, -1):
        pl.semaphore_signal(
            relay_x_sem, inc=1, device_id=device(0, way, 0), device_id_type=MESH
        )
    send_rows(0, 2)
    send_nd(0, 2)

    pl.semaphore_wait(relay_x_sem, 2)
    for tx in (1, -1):
        for ty in (1, -1, 2):
            send_rows(tx, ty)
            send_nd(tx, ty)
    ring_step(2)
    if half > 2:
        ring_step(3)
    for sy in (0, 1):
        wait_chunk(-1, sy)
        forward(-1, sy, 1)
    for sy in (-1, 2):
        wait_chunk(1, sy)
        forward(1, sy, -1)
    qlane = lax.broadcasted_iota(jnp.int32, (1, rows), 1)
    qpos = jnp.zeros((1, rows), jnp.int32)
    for chunk in range(plane):
        qpos = jnp.where(qlane // QCHUNK == chunk, query_order[my_z * plane + chunk], qpos)
    offset = key_order.shape[0] * KCHUNK - query_order.shape[0] * QCHUNK
    qpos = offset + qpos * QCHUNK + qlane % QCHUNK
    low = jnp.zeros((1, rows), jnp.int32)
    high = jnp.zeros((1, rows), jnp.int32)
    for row in range(table.shape[1]):
        inside = (qpos >= table[0, row]) & (qpos < table[1, row])
        last = jnp.where(table[4, row] != 0, jnp.minimum(table[3, row], qpos + 1), table[3, row])
        low = jnp.where(inside, table[2, row], low)
        high = jnp.where(inside, last, high)
    krow = lax.broadcasted_iota(jnp.int32, (KCHUNK, rows), 0)
    dq_acc[...] = jnp.zeros_like(dq_acc)

    for step in range(4, half + 1):
        ring_step(step)
    for sy in (1, 2, -1):
        wait_chunk(0, sy)
    for sy in (0, 1):
        wait_chunk(1, sy)
    for sy in (-1, 2):
        wait_chunk(-1, sy)
    for sy in range(size_y):
        wait_chunk(2, sy)
    for copy in own_copies:
        copy.wait()
    turned = nd_all[...].T
    nd_rows[...] = turned[0 : 2 * heads_all]

    order = [0, half]
    for distance in range(half - 1, 0, -1):
        order += [distance, -distance]

    def by_head(first):
        return jnp.concatenate(
            [qg_all[:, pl.ds(first + head * HEAD_DIM, HEAD_DIM)] for head in range(heads_loc)],
            axis=0,
        )

    def block_terms(index, dist):
        zb = ring_z(dist)
        first = (zb * size_x + my_x) * DISPATCH
        for part in range(DISPATCH):
            base = key_order[first + part] * KCHUNK
            ok = (krow >= low - base) & (krow < high - base)
            bias[pl.ds(part * KCHUNK, KCHUNK), :] = jnp.where(ok, jnp.inf, -jnp.inf).astype(F32)
        key_blk = k_all[zb]
        value_blk = v_all[zb]
        weights_low = []
        dscores = []
        for head in range(heads_loc):
            cols = pl.ds(head * HEAD_DIM, HEAD_DIM)
            norm = nd_rows[pl.ds(my_y * heads_loc + head, 1), :]
            delta = nd_rows[pl.ds(heads_all + my_y * heads_loc + head, 1), :]
            scores = dot_nt(key_blk, qg_all[:, cols])
            weights = jnp.exp2(jnp.minimum(scores * (score_scale * log2e) - norm, bias[...]))
            dprobs = dot_nt(value_blk, qg_all[:, pl.ds(width + head * HEAD_DIM, HEAD_DIM)])
            weights_low.append(weights.astype(BF16))
            dscores.append((weights * (dprobs - delta)).astype(BF16))
        part_v[index] = dot_nn(jnp.concatenate(weights_low, axis=1), by_head(width))
        part_k[index] = dot_nn(jnp.concatenate(dscores, axis=1), by_head(0))
        key_turned = key_blk.T
        for head in range(heads_loc):
            dq_acc[:, pl.ds(head * rows, rows)] += dot_nn(key_turned, dscores[head])

    lines = {("k", 1): half, ("v", -1): half, ("v", 1): half - 1, ("k", -1): half - 1}
    slots = {}
    for (kind, way), first_dist in lines.items():
        for dist in range(first_dist, 0, -1):
            slots[(kind, way, dist)] = len(slots)

    def chain_copy(kind, way, dist):
        slot = slots[(kind, way, dist)]
        dst = chain_recv.at[slot]
        if dist == 1:
            dst = (recv_k if kind == "k" else recv_v).at[0 if way == 1 else 1]
        return pltpu.make_async_remote_copy(
            src_ref=chain_send.at[slot],
            dst_ref=dst,
            send_sem=chain_send_sem.at[slot],
            recv_sem=chain_recv_sem.at[slot],
            device_id=z_device(2 * way if dist == half else way),
            device_id_type=MESH,
        )

    def chain_step(kind, way, dist):
        index = order.index(half if dist == half else way * dist)
        value = (part_k if kind == "k" else part_v)[index]
        joined = [dist + 1] if dist < half - 1 else []
        if dist == half - 2 and (kind, way, half) in slots:
            joined.append(half)
        for earlier in joined:
            chain_copy(kind, way, earlier).wait_recv()
            value = value + chain_recv[slots[(kind, way, earlier)]].astype(F32)
        chain_send[slots[(kind, way, dist)]] = value.astype(BF16)
        chain_copy(kind, way, dist).start()

    events = {at: [] for at in range(size_z + 1)}
    events[1] = [("k", 1, 4), ("v", -1, 4)]
    events[2] = [("k", 1, 3)]
    events[3] = [("v", -1, 3), ("v", 1, 3), ("k", -1, 3)]
    events[6] = [("k", 1, 2), ("v", -1, 2)]
    events[7] = [("v", 1, 2), ("k", -1, 2)]
    events[8] = [("k", 1, 1), ("v", -1, 1), ("v", 1, 1), ("k", -1, 1)]

    def dist_at(index):
        near = half - index // 2
        paired = jnp.where(index % 2 == 0, near, -near)
        return jnp.where(index == 0, 0, jnp.where(index == 1, half, paired))

    def block_step(index, carry):
        @pl.when(index == 1)
        def _():
            ring_step(half + 1)

        block_terms(index, dist_at(index))

        for at in range(1, size_z):
            if events[at]:

                @pl.when(index == at)
                def _(at=at):
                    for event in events[at]:
                        chain_step(*event)

        return carry

    lax.fori_loop(0, size_z, block_step, 0)

    stores = [
        pltpu.make_async_copy(part_k.at[0], own_k, store_sem.at[0]),
        pltpu.make_async_copy(part_v.at[0], own_v, store_sem.at[1]),
    ]
    for copy in stores:
        copy.start()

    peers = [(dx, dy) for dx in range(size_x) for dy in range(size_y) if dx or dy]
    peers.sort(key=lambda p: -(min(p[0], size_x - p[0]) + min(p[1], size_y - p[1])))
    for head in range(heads_loc):
        turned = dq_acc[:, pl.ds(head * rows, rows)].T
        dq_send[:, pl.ds(head * HEAD_DIM, HEAD_DIM)] = turned.astype(BF16)
    for dx, dy in peers:
        pltpu.make_async_remote_copy(
            src_ref=dq_send.at[chunk_rows(dx, dy)],
            dst_ref=dq_recv.at[my_x, :, my_cols],
            send_sem=dq_send_sem,
            recv_sem=dq_recv_sem,
            device_id=device(0, dx, dy),
            device_id_type=MESH,
        ).start()
    pltpu.make_async_copy(
        dq_send.at[my_rows], dq_recv.at[my_x, :, my_cols], dq_recv_sem
    ).start()

    for event in events[size_z]:
        chain_step(*event)

    pltpu.make_async_copy(dq_recv, dq_recv, dq_recv_sem).wait()
    for key in slots:
        if key[2] == 1:
            chain_copy(*key).wait_recv()

    for copy in ring.values():
        copy.wait_send()
    for key in slots:
        chain_copy(*key).wait_send()
    sent = pl.ds(0, len(peers) * QCHUNK)
    pltpu.make_async_copy(qg_all.at[sent], qg_all.at[sent], qg_send_sem).wait()
    pltpu.make_async_copy(nd_all.at[sent], nd_all.at[sent], nd_send_sem).wait()
    pltpu.make_async_copy(dq_send.at[sent], dq_send.at[sent], dq_send_sem).wait()
    for copy in stores:
        copy.wait()


def add_up_kernel(dq_recv, own_k, own_v, recv_k, recv_v, dq_out, dk_out, dv_out):
    score_scale = 1.0 / math.sqrt(HEAD_DIM)
    total = dq_recv[0].astype(F32)
    for other in range(1, dq_recv.shape[0]):
        total = total + dq_recv[other].astype(F32)
    dq_out[...] = (total * score_scale).astype(BF16)
    total = own_k[...] + recv_k[0].astype(F32) + recv_k[1].astype(F32)
    dk_out[...] = (total * score_scale).astype(BF16)
    total = own_v[...] + recv_v[0].astype(F32) + recv_v[1].astype(F32)
    dv_out[...] = total.astype(BF16)


def add_up(terms):
    vmem = pl.BlockSpec(memory_space=pltpu.VMEM)
    dq_recv, own_k, own_v = terms[:3]
    return pl.pallas_call(
        add_up_kernel,
        out_shape=(
            jax.ShapeDtypeStruct(dq_recv.shape[1:], BF16),
            jax.ShapeDtypeStruct(own_k.shape, BF16),
            jax.ShapeDtypeStruct(own_v.shape, BF16),
        ),
        in_specs=[vmem] * 5,
        out_specs=(vmem,) * 3,
        name="add_up",
        compiler_params=pltpu.CompilerParams(vmem_limit_bytes=60 * 1024 * 1024),
    )(*terms)


def local(
    sizes,
    query_rows,
    key_rows,
    value_rows,
    output_rows,
    grad_out,
    log_norm,
    mask_table,
    key_order,
    query_order,
):
    size_z, size_x, size_y = sizes
    half = size_z // 2
    rows = size_x * size_y * QCHUNK
    key_count = key_rows.shape[0]
    own, columns = query_rows.shape
    heads_all = log_norm.shape[1]
    width = columns // size_y
    chain = 2 * (2 * half - 1)
    hbm = pl.BlockSpec(memory_space=pltpu.HBM)
    dma = pltpu.SemaphoreType.DMA
    terms = pl.pallas_call(
        functools.partial(kernel, sizes),
        out_shape=(
            jax.ShapeDtypeStruct((size_x,) + query_rows.shape, BF16),
            jax.ShapeDtypeStruct(key_rows.shape, F32),
            jax.ShapeDtypeStruct(value_rows.shape, F32),
            jax.ShapeDtypeStruct((2,) + key_rows.shape, BF16),
            jax.ShapeDtypeStruct((2,) + value_rows.shape, BF16),
        ),
        in_specs=[hbm] * 9,
        out_specs=(hbm,) * 5,
        scratch_shapes=[
            pltpu.VMEM((rows, 2 * width), BF16),
            pltpu.VMEM((rows, 128), F32),
            pltpu.VMEM((size_z, key_count, HEAD_DIM), BF16),
            pltpu.VMEM((size_z, key_count, HEAD_DIM), BF16),
            pltpu.VMEM((own, columns), BF16),
            pltpu.VMEM((own, columns), BF16),
            pltpu.VMEM((own, heads_all), F32),
            pltpu.VMEM((own, 128), F32),
            pltpu.VMEM((2 * heads_all, rows), F32),
            pltpu.SMEM(mask_table.shape[::-1], jnp.int32),
            pltpu.SMEM(key_order.shape, jnp.int32),
            pltpu.SMEM(query_order.shape, jnp.int32),
            pltpu.VMEM((key_count, rows), F32),
            pltpu.VMEM((HEAD_DIM, width // HEAD_DIM * rows), F32),
            pltpu.VMEM((rows, width), BF16),
            pltpu.VMEM((size_z, key_count, HEAD_DIM), F32),
            pltpu.VMEM((size_z, key_count, HEAD_DIM), F32),
            pltpu.VMEM((chain, key_count, HEAD_DIM), BF16),
            pltpu.VMEM((chain, key_count, HEAD_DIM), BF16),
            dma((8,)),
            dma((3,)),
            pltpu.SemaphoreType.REGULAR,
            pltpu.SemaphoreType.REGULAR,
            dma,
            dma,
            dma((size_x * size_y,)),
            dma((size_x * size_y,)),
            dma((chain,)),
            dma((chain,)),
            dma((chain,)),
            dma((chain,)),
            dma,
            dma,
            dma((2,)),
        ],
        compiler_params=pltpu.CompilerParams(
            collective_id=0, has_side_effects=True, vmem_limit_bytes=60 * 1024 * 1024
        ),
    )(
        query_rows,
        key_rows,
        value_rows,
        output_rows,
        grad_out,
        log_norm,
        mask_table.T,
        key_order,
        query_order,
    )
    return add_up(terms)


def solution(mesh, ring_x=RING_X):
    sizes = (mesh.shape["ctx"] // ring_x, ring_x, mesh.shape["head"])
    return jax.shard_map(
        functools.partial(local, sizes),
        mesh=mesh,
        in_specs=(
            P(("dp", "ctx", "head"), None),
            P(("dp", "ctx"), "head"),
            P(("dp", "ctx"), "head"),
            P(("dp", "ctx", "head"), None),
            P(("dp", "ctx", "head"), None),
            P(("dp", "ctx", "head"), None),
            P("dp", None),
            P("dp"),
            P("dp"),
        ),
        out_specs=(
            P(("dp", "ctx", "head"), None),
            P(("dp", "ctx"), "head"),
            P(("dp", "ctx"), "head"),
        ),
        check_vma=False,
    )
```

```python
import functools
import math

import jax
import jax.numpy as jnp
from jax import lax
from jax.experimental import pallas as pl
from jax.experimental.pallas import tpu as pltpu
from jax.sharding import PartitionSpec as P

HEAD_DIM = 128
DISPATCH = 4
KCHUNK = 64
QCHUNK = 16
RING_X = 4
MESH = pl.DeviceIdType.MESH
F32 = jnp.float32
BF16 = jnp.bfloat16


def dot_nt(lhs, rhs):
    return lax.dot_general(lhs, rhs, (((1,), (1,)), ((), ())), preferred_element_type=F32)


def dot_nn(lhs, rhs):
    return lax.dot_general(lhs, rhs, (((1,), (0,)), ((), ())), preferred_element_type=F32)


def kernel(
    sizes,
    q_hbm,
    k_hbm,
    v_hbm,
    o_hbm,
    g_hbm,
    norm_hbm,
    table_hbm,
    key_order_hbm,
    query_order_hbm,
    dq_recv,
    own_k,
    own_v,
    recv_k,
    recv_v,
    qg_all,
    nd_all,
    k_all,
    v_all,
    o_own,
    g_own,
    norm_own,
    nd_own,
    nd_rows,
    table,
    key_order,
    query_order,
    bias,
    dq_acc,
    dq_send,
    part_k,
    part_v,
    chain_send,
    chain_recv,
    load_sem,
    own_sem,
    relay_sem,
    relay_x_sem,
    qg_send_sem,
    nd_send_sem,
    qg_recv_sem,
    nd_recv_sem,
    ring_send,
    ring_recv,
    chain_send_sem,
    chain_recv_sem,
    dq_send_sem,
    dq_recv_sem,
    store_sem,
):
    size_z, size_x, size_y = sizes
    half = size_z // 2
    plane = size_x * size_y
    rows = plane * QCHUNK
    key_count = k_hbm.shape[0]
    heads_all = norm_hbm.shape[1]
    heads_loc = heads_all // size_y
    width = heads_loc * HEAD_DIM
    score_scale = 1.0 / math.sqrt(HEAD_DIM)
    log2e = math.log2(math.e)

    ctx = lax.axis_index("ctx")
    my_y = lax.axis_index("head")
    my_z = ctx // size_x
    my_x = ctx % size_x
    me = my_x * size_y + my_y
    my_rows = pl.ds(pl.multiple_of(me * QCHUNK, QCHUNK), QCHUNK)
    my_cols = pl.ds(pl.multiple_of(my_y * width, 128), width)

    def ring_z(offset):
        return (my_z + offset + size_z) % size_z

    def device(dz, dx, dy):
        return {
            "ctx": ring_z(dz) * size_x + (my_x + dx + size_x) % size_x,
            "head": (my_y + dy + size_y) % size_y,
        }

    def z_device(offset):
        return device(offset, 0, 0)

    def chunk_rows(sx, sy):
        chunk = (my_x + sx + size_x) % size_x * size_y + (my_y + sy + size_y) % size_y
        return pl.ds(pl.multiple_of(chunk * QCHUNK, QCHUNK), QCHUNK)

    barrier = pltpu.get_barrier_semaphore()
    neighbours = [(1, 0, 0), (-1, 0, 0), (0, 1, 0), (0, -1, 0), (0, 0, 1), (0, 0, -1)]
    for neighbour in neighbours:
        pl.semaphore_signal(
            barrier, inc=1, device_id=device(*neighbour), device_id_type=MESH
        )

    pl.semaphore_wait(barrier, len(neighbours))

    def ring_copy(ref, way, step, index):
        slot = ring_z(-way * (step - 1))
        src = ref.at[slot] if step > 1 else (k_hbm if ref is k_all else v_hbm)
        return pltpu.make_async_remote_copy(
            src_ref=src,
            dst_ref=ref.at[slot],
            send_sem=ring_send.at[index],
            recv_sem=ring_recv.at[index],
            device_id=z_device(way),
            device_id_type=MESH,
        )

    ring_plan = []
    for ref, way, steps in (
        (k_all, 1, half),
        (v_all, -1, half),
        (v_all, 1, half - 1),
        (k_all, -1, half - 1),
    ):
        ring_plan.append((ref, way, steps))
    ring = {}
    count = 0
    for step in range(1, half + 1):
        for line, (ref, way, steps) in enumerate(ring_plan):
            if step <= steps:
                ring[(line, step)] = ring_copy(ref, way, step, count)
                count += 1
    for line in range(4):
        if (line, 1) in ring:
            ring[(line, 1)].start()

    for way in (1, -1):
        pl.semaphore_signal(
            relay_sem, inc=1, device_id=device(0, 0, way), device_id_type=MESH
        )

    loads = [
        pltpu.make_async_copy(k_hbm, k_all.at[my_z], load_sem.at[0]),
        pltpu.make_async_copy(v_hbm, v_all.at[my_z], load_sem.at[1]),
        pltpu.make_async_copy(g_hbm, g_own, load_sem.at[2]),
        pltpu.make_async_copy(o_hbm, o_own, load_sem.at[3]),
        pltpu.make_async_copy(norm_hbm, norm_own, load_sem.at[4]),
        pltpu.make_async_copy(table_hbm, table, load_sem.at[5]),
        pltpu.make_async_copy(key_order_hbm, key_order, load_sem.at[6]),
        pltpu.make_async_copy(query_order_hbm, query_order, load_sem.at[7]),
    ]
    for copy in loads:
        copy.start()

    def slot_of(sx, sy):
        return (sx + 2 * size_x) % size_x * size_y + (sy + 2 * size_y) % size_y

    def plane_copy(src, dst, sends, receives, tx, ty, sx, sy):
        slot = slot_of(sx - tx, sy - ty)
        pltpu.make_async_remote_copy(
            src_ref=src,
            dst_ref=dst,
            send_sem=sends,
            recv_sem=receives.at[slot],
            device_id=device(0, tx, ty),
            device_id_type=MESH,
        ).start()

    def send_rows(tx, ty):
        group = (my_y + ty + size_y) % size_y
        cols = pl.ds(pl.multiple_of(group * width, 128), width)
        for part, src in enumerate((q_hbm, g_hbm)):
            plane_copy(
                src.at[:, cols],
                qg_all.at[my_rows, pl.ds(part * width, width)],
                qg_send_sem,
                qg_recv_sem,
                tx,
                ty,
                0,
                0,
            )

    def send_nd(tx, ty):
        plane_copy(nd_own, nd_all.at[my_rows], nd_send_sem, nd_recv_sem, tx, ty, 0, 0)

    def wait_chunk(sx, sy):
        at = chunk_rows(sx, sy)
        slot = slot_of(sx, sy)
        pltpu.make_async_copy(qg_all.at[at], qg_all.at[at], qg_recv_sem.at[slot]).wait()
        pltpu.make_async_copy(nd_all.at[at], nd_all.at[at], nd_recv_sem.at[slot]).wait()

    def forward(sx, sy, way):
        at = chunk_rows(sx, sy)
        plane_copy(qg_all.at[at], qg_all.at[at], qg_send_sem, qg_recv_sem, way, 0, sx, sy)
        plane_copy(nd_all.at[at], nd_all.at[at], nd_send_sem, nd_recv_sem, way, 0, sx, sy)

    def ring_step(step):
        for line in range(4):
            if (line, step - 1) in ring:
                ring[(line, step - 1)].wait_recv()
            if (line, step) in ring:
                ring[(line, step)].start()

    beside = ((0, 1), (0, -1), (1, 0), (-1, 0))
    for peer in beside:
        send_rows(*peer)
    own_copies = [
        pltpu.make_async_copy(
            q_hbm.at[:, my_cols], qg_all.at[my_rows, pl.ds(0, width)], own_sem.at[1]
        ),
        pltpu.make_async_copy(
            g_hbm.at[:, my_cols], qg_all.at[my_rows, pl.ds(width, width)], own_sem.at[2]
        ),
    ]
    for copy in own_copies:
        copy.start()

    for copy in loads:
        copy.wait()

    lane = lax.broadcasted_iota(jnp.int32, (QCHUNK, 128), 1)
    tile = jnp.zeros((QCHUNK, 128), F32)
    for head in range(heads_all):
        cols = pl.ds(head * HEAD_DIM, HEAD_DIM)
        delta = jnp.sum(
            g_own[:, cols].astype(F32) * o_own[:, cols].astype(F32), axis=1, keepdims=True
        )
        tile = jnp.where(lane == heads_all + head, delta, tile)
    nd_own[...] = tile
    nd_own[:, 0:heads_all] = norm_own[...] * log2e

    for peer in beside:
        send_nd(*peer)
    own_copies.append(pltpu.make_async_copy(nd_own, nd_all.at[my_rows], own_sem.at[0]))
    own_copies[-1].start()
    pl.semaphore_wait(relay_sem, 2)
    for way in (1, -1):
        pl.semaphore_signal(
            relay_x_sem, inc=1, device_id=device(0, way, 0), device_id_type=MESH
        )
    send_rows(0, 2)
    send_nd(0, 2)

    pl.semaphore_wait(relay_x_sem, 2)
    for tx in (1, -1):
        for ty in (1, -1, 2):
            send_rows(tx, ty)
            send_nd(tx, ty)
    ring_step(2)
    if half > 2:
        ring_step(3)
    for sy in (0, 1):
        wait_chunk(-1, sy)
        forward(-1, sy, 1)
    for sy in (-1, 2):
        wait_chunk(1, sy)
        forward(1, sy, -1)
    qlane = lax.broadcasted_iota(jnp.int32, (1, rows), 1)
    qpos = jnp.zeros((1, rows), jnp.int32)
    for chunk in range(plane):
        qpos = jnp.where(qlane // QCHUNK == chunk, query_order[my_z * plane + chunk], qpos)
    offset = key_order.shape[0] * KCHUNK - query_order.shape[0] * QCHUNK
    qpos = offset + qpos * QCHUNK + qlane % QCHUNK
    low = jnp.zeros((1, rows), jnp.int32)
    high = jnp.zeros((1, rows), jnp.int32)
    for row in range(table.shape[1]):
        inside = (qpos >= table[0, row]) & (qpos < table[1, row])
        last = jnp.where(table[4, row] != 0, jnp.minimum(table[3, row], qpos + 1), table[3, row])
        low = jnp.where(inside, table[2, row], low)
        high = jnp.where(inside, last, high)
    krow = lax.broadcasted_iota(jnp.int32, (KCHUNK, rows), 0)
    dq_acc[...] = jnp.zeros_like(dq_acc)

    for step in range(4, half + 1):
        ring_step(step)
    for sy in (1, 2, -1):
        wait_chunk(0, sy)
    for sy in (0, 1):
        wait_chunk(1, sy)
    for sy in (-1, 2):
        wait_chunk(-1, sy)
    for sy in range(size_y):
        wait_chunk(2, sy)
    for copy in own_copies:
        copy.wait()
    turned = nd_all[...].T
    nd_rows[...] = turned[0 : 2 * heads_all]

    order = [0, half]
    for distance in range(half - 1, 0, -1):
        order += [distance, -distance]

    def by_head(first):
        return jnp.concatenate(
            [qg_all[:, pl.ds(first + head * HEAD_DIM, HEAD_DIM)] for head in range(heads_loc)],
            axis=0,
        )

    def block_terms(index, dist):
        zb = ring_z(dist)
        first = (zb * size_x + my_x) * DISPATCH
        for part in range(DISPATCH):
            base = key_order[first + part] * KCHUNK
            ok = (krow >= low - base) & (krow < high - base)
            bias[pl.ds(part * KCHUNK, KCHUNK), :] = jnp.where(ok, jnp.inf, -jnp.inf).astype(F32)
        key_blk = k_all[zb]
        value_blk = v_all[zb]
        weights_low = []
        dscores = []
        for head in range(heads_loc):
            cols = pl.ds(head * HEAD_DIM, HEAD_DIM)
            norm = nd_rows[pl.ds(my_y * heads_loc + head, 1), :]
            delta = nd_rows[pl.ds(heads_all + my_y * heads_loc + head, 1), :]
            scores = dot_nt(key_blk, qg_all[:, cols])
            weights = jnp.exp2(jnp.minimum(scores * (score_scale * log2e) - norm, bias[...]))
            dprobs = dot_nt(value_blk, qg_all[:, pl.ds(width + head * HEAD_DIM, HEAD_DIM)])
            weights_low.append(weights.astype(BF16))
            dscores.append((weights * (dprobs - delta)).astype(BF16))
        part_v[index] = dot_nn(jnp.concatenate(weights_low, axis=1), by_head(width))
        part_k[index] = dot_nn(jnp.concatenate(dscores, axis=1), by_head(0))
        key_turned = key_blk.T
        for head in range(heads_loc):
            dq_acc[:, pl.ds(head * rows, rows)] += dot_nn(key_turned, dscores[head])

    lines = {("k", 1): half, ("v", -1): half, ("v", 1): half - 1, ("k", -1): half - 1}
    slots = {}
    for (kind, way), first_dist in lines.items():
        for dist in range(first_dist, 0, -1):
            slots[(kind, way, dist)] = len(slots)

    def chain_copy(kind, way, dist):
        slot = slots[(kind, way, dist)]
        dst = chain_recv.at[slot]
        if dist == 1:
            dst = (recv_k if kind == "k" else recv_v).at[0 if way == 1 else 1]
        return pltpu.make_async_remote_copy(
            src_ref=chain_send.at[slot],
            dst_ref=dst,
            send_sem=chain_send_sem.at[slot],
            recv_sem=chain_recv_sem.at[slot],
            device_id=z_device(2 * way if dist == half else way),
            device_id_type=MESH,
        )

    def chain_step(kind, way, dist):
        index = order.index(half if dist == half else way * dist)
        value = (part_k if kind == "k" else part_v)[index]
        joined = [dist + 1] if dist < half - 1 else []
        if dist == half - 2 and (kind, way, half) in slots:
            joined.append(half)
        for earlier in joined:
            chain_copy(kind, way, earlier).wait_recv()
            value = value + chain_recv[slots[(kind, way, earlier)]].astype(F32)
        chain_send[slots[(kind, way, dist)]] = value.astype(BF16)
        chain_copy(kind, way, dist).start()

    events = {at: [] for at in range(size_z + 1)}
    events[1] = [("k", 1, 4), ("v", -1, 4)]
    events[2] = [("v", 1, 3)]
    events[3] = [("k", -1, 3), ("k", 1, 3), ("v", -1, 3)]
    events[6] = [("v", 1, 2), ("k", -1, 2)]
    events[7] = [("k", 1, 2), ("v", -1, 2)]
    events[8] = [("v", 1, 1), ("k", -1, 1), ("k", 1, 1), ("v", -1, 1)]

    def dist_at(index):
        near = half - index // 2
        paired = jnp.where(index % 2 == 0, near, -near)
        return jnp.where(index == 0, 0, jnp.where(index == 1, half, paired))

    def block_step(index, carry):
        @pl.when(index == 1)
        def _():
            ring_step(half + 1)

        block_terms(index, dist_at(index))

        for at in range(1, size_z):
            if events[at]:

                @pl.when(index == at)
                def _(at=at):
                    for event in events[at]:
                        chain_step(*event)

        return carry

    lax.fori_loop(0, size_z, block_step, 0)

    stores = [
        pltpu.make_async_copy(part_k.at[0], own_k, store_sem.at[0]),
        pltpu.make_async_copy(part_v.at[0], own_v, store_sem.at[1]),
    ]
    for copy in stores:
        copy.start()

    peers = [(dx, dy) for dx in range(size_x) for dy in range(size_y) if dx or dy]
    peers.sort(key=lambda p: -(min(p[0], size_x - p[0]) + min(p[1], size_y - p[1])))
    for head in range(heads_loc):
        turned = dq_acc[:, pl.ds(head * rows, rows)].T
        dq_send[:, pl.ds(head * HEAD_DIM, HEAD_DIM)] = turned.astype(BF16)
    for dx, dy in peers:
        pltpu.make_async_remote_copy(
            src_ref=dq_send.at[chunk_rows(dx, dy)],
            dst_ref=dq_recv.at[my_x, :, my_cols],
            send_sem=dq_send_sem,
            recv_sem=dq_recv_sem,
            device_id=device(0, dx, dy),
            device_id_type=MESH,
        ).start()
    pltpu.make_async_copy(
        dq_send.at[my_rows], dq_recv.at[my_x, :, my_cols], dq_recv_sem
    ).start()

    for event in events[size_z]:
        chain_step(*event)

    pltpu.make_async_copy(dq_recv, dq_recv, dq_recv_sem).wait()
    for key in slots:
        if key[2] == 1:
            chain_copy(*key).wait_recv()

    for copy in ring.values():
        copy.wait_send()
    for key in slots:
        chain_copy(*key).wait_send()
    sent = pl.ds(0, len(peers) * QCHUNK)
    pltpu.make_async_copy(qg_all.at[sent], qg_all.at[sent], qg_send_sem).wait()
    pltpu.make_async_copy(nd_all.at[sent], nd_all.at[sent], nd_send_sem).wait()
    pltpu.make_async_copy(dq_send.at[sent], dq_send.at[sent], dq_send_sem).wait()
    for copy in stores:
        copy.wait()


def add_up_kernel(dq_recv, own_k, own_v, recv_k, recv_v, dq_out, dk_out, dv_out):
    score_scale = 1.0 / math.sqrt(HEAD_DIM)
    total = dq_recv[0].astype(F32)
    for other in range(1, dq_recv.shape[0]):
        total = total + dq_recv[other].astype(F32)
    dq_out[...] = (total * score_scale).astype(BF16)
    total = own_k[...] + recv_k[0].astype(F32) + recv_k[1].astype(F32)
    dk_out[...] = (total * score_scale).astype(BF16)
    total = own_v[...] + recv_v[0].astype(F32) + recv_v[1].astype(F32)
    dv_out[...] = total.astype(BF16)


def add_up(terms):
    vmem = pl.BlockSpec(memory_space=pltpu.VMEM)
    dq_recv, own_k, own_v = terms[:3]
    return pl.pallas_call(
        add_up_kernel,
        out_shape=(
            jax.ShapeDtypeStruct(dq_recv.shape[1:], BF16),
            jax.ShapeDtypeStruct(own_k.shape, BF16),
            jax.ShapeDtypeStruct(own_v.shape, BF16),
        ),
        in_specs=[vmem] * 5,
        out_specs=(vmem,) * 3,
        name="add_up",
        compiler_params=pltpu.CompilerParams(vmem_limit_bytes=32 * 1024 * 1024),
    )(*(pltpu.with_memory_space_constraint(term, pltpu.VMEM) for term in terms))


def local(
    sizes,
    query_rows,
    key_rows,
    value_rows,
    output_rows,
    grad_out,
    log_norm,
    mask_table,
    key_order,
    query_order,
):
    size_z, size_x, size_y = sizes
    half = size_z // 2
    rows = size_x * size_y * QCHUNK
    key_count = key_rows.shape[0]
    own, columns = query_rows.shape
    heads_all = log_norm.shape[1]
    width = columns // size_y
    chain = 2 * (2 * half - 1)
    hbm = pl.BlockSpec(memory_space=pltpu.HBM)
    dma = pltpu.SemaphoreType.DMA
    terms = pl.pallas_call(
        functools.partial(kernel, sizes),
        out_shape=(
            pltpu.VMEM((size_x,) + query_rows.shape, BF16),
            pltpu.VMEM(key_rows.shape, F32),
            pltpu.VMEM(value_rows.shape, F32),
            pltpu.VMEM((2,) + key_rows.shape, BF16),
            pltpu.VMEM((2,) + value_rows.shape, BF16),
        ),
        in_specs=[hbm] * 9,
        out_specs=(pl.BlockSpec(memory_space=pltpu.VMEM),) * 5,
        scratch_shapes=[
            pltpu.VMEM((rows, 2 * width), BF16),
            pltpu.VMEM((rows, 128), F32),
            pltpu.VMEM((size_z, key_count, HEAD_DIM), BF16),
            pltpu.VMEM((size_z, key_count, HEAD_DIM), BF16),
            pltpu.VMEM((own, columns), BF16),
            pltpu.VMEM((own, columns), BF16),
            pltpu.VMEM((own, heads_all), F32),
            pltpu.VMEM((own, 128), F32),
            pltpu.VMEM((2 * heads_all, rows), F32),
            pltpu.SMEM(mask_table.shape[::-1], jnp.int32),
            pltpu.SMEM(key_order.shape, jnp.int32),
            pltpu.SMEM(query_order.shape, jnp.int32),
            pltpu.VMEM((key_count, rows), F32),
            pltpu.VMEM((HEAD_DIM, width // HEAD_DIM * rows), F32),
            pltpu.VMEM((rows, width), BF16),
            pltpu.VMEM((size_z, key_count, HEAD_DIM), F32),
            pltpu.VMEM((size_z, key_count, HEAD_DIM), F32),
            pltpu.VMEM((chain, key_count, HEAD_DIM), BF16),
            pltpu.VMEM((chain, key_count, HEAD_DIM), BF16),
            dma((8,)),
            dma((3,)),
            pltpu.SemaphoreType.REGULAR,
            pltpu.SemaphoreType.REGULAR,
            dma,
            dma,
            dma((size_x * size_y,)),
            dma((size_x * size_y,)),
            dma((chain,)),
            dma((chain,)),
            dma((chain,)),
            dma((chain,)),
            dma,
            dma,
            dma((2,)),
        ],
        compiler_params=pltpu.CompilerParams(
            collective_id=0, has_side_effects=True, vmem_limit_bytes=32 * 1024 * 1024
        ),
    )(
        *(
            pltpu.with_memory_space_constraint(operand, pltpu.HBM)
            for operand in (
                query_rows,
                key_rows,
                value_rows,
                output_rows,
                grad_out,
                log_norm,
                mask_table.T,
                key_order,
                query_order,
            )
        )
    )
    return add_up(terms)


def solution(mesh, ring_x=RING_X):
    sizes = (mesh.shape["ctx"] // ring_x, ring_x, mesh.shape["head"])
    return jax.shard_map(
        functools.partial(local, sizes),
        mesh=mesh,
        in_specs=(
            P(("dp", "ctx", "head"), None),
            P(("dp", "ctx"), "head"),
            P(("dp", "ctx"), "head"),
            P(("dp", "ctx", "head"), None),
            P(("dp", "ctx", "head"), None),
            P(("dp", "ctx", "head"), None),
            P("dp", None),
            P("dp"),
            P("dp"),
        ),
        out_specs=(
            P(("dp", "ctx", "head"), None),
            P(("dp", "ctx"), "head"),
            P(("dp", "ctx"), "head"),
        ),
        check_vma=False,
    )
```

```python
import functools
import math

import jax
import jax.numpy as jnp
from jax import lax
from jax.experimental import pallas as pl
from jax.experimental.pallas import tpu as pltpu
from jax.sharding import PartitionSpec as P

HEAD_DIM = 128
DISPATCH = 4
KCHUNK = 64
QCHUNK = 16
RING_X = 4
MESH = pl.DeviceIdType.MESH
F32 = jnp.float32
BF16 = jnp.bfloat16


def dot_nt(lhs, rhs):
    return lax.dot_general(lhs, rhs, (((1,), (1,)), ((), ())), preferred_element_type=F32)


def dot_nn(lhs, rhs):
    return lax.dot_general(lhs, rhs, (((1,), (0,)), ((), ())), preferred_element_type=F32)


def kernel(
    sizes,
    q_hbm,
    k_hbm,
    v_hbm,
    o_hbm,
    g_hbm,
    norm_hbm,
    table_hbm,
    key_order_hbm,
    query_order_hbm,
    dq_recv,
    own_k,
    own_v,
    recv_k,
    recv_v,
    qg_all,
    nd_all,
    k_all,
    v_all,
    o_own,
    g_own,
    norm_own,
    nd_own,
    nd_rows,
    table,
    key_order,
    query_order,
    bias,
    dq_acc,
    dq_send,
    part_k,
    part_v,
    chain_send,
    chain_recv,
    load_sem,
    own_sem,
    relay_sem,
    relay_x_sem,
    qg_send_sem,
    nd_send_sem,
    qg_recv_sem,
    nd_recv_sem,
    ring_send,
    ring_recv,
    chain_send_sem,
    chain_recv_sem,
    dq_send_sem,
    dq_recv_sem,
    store_sem,
):
    size_z, size_x, size_y = sizes
    half = size_z // 2
    plane = size_x * size_y
    rows = plane * QCHUNK
    key_count = k_hbm.shape[0]
    heads_all = norm_hbm.shape[1]
    heads_loc = heads_all // size_y
    width = heads_loc * HEAD_DIM
    score_scale = 1.0 / math.sqrt(HEAD_DIM)
    log2e = math.log2(math.e)

    ctx = lax.axis_index("ctx")
    my_y = lax.axis_index("head")
    my_z = ctx // size_x
    my_x = ctx % size_x
    me = my_x * size_y + my_y
    my_rows = pl.ds(pl.multiple_of(me * QCHUNK, QCHUNK), QCHUNK)
    my_cols = pl.ds(pl.multiple_of(my_y * width, 128), width)

    def ring_z(offset):
        return (my_z + offset + size_z) % size_z

    def device(dz, dx, dy):
        return {
            "ctx": ring_z(dz) * size_x + (my_x + dx + size_x) % size_x,
            "head": (my_y + dy + size_y) % size_y,
        }

    def z_device(offset):
        return device(offset, 0, 0)

    def chunk_rows(sx, sy):
        chunk = (my_x + sx + size_x) % size_x * size_y + (my_y + sy + size_y) % size_y
        return pl.ds(pl.multiple_of(chunk * QCHUNK, QCHUNK), QCHUNK)

    barrier = pltpu.get_barrier_semaphore()
    neighbours = [(1, 0, 0), (-1, 0, 0), (0, 1, 0), (0, -1, 0), (0, 0, 1), (0, 0, -1)]
    for neighbour in neighbours:
        pl.semaphore_signal(
            barrier, inc=1, device_id=device(*neighbour), device_id_type=MESH
        )

    pl.semaphore_wait(barrier, len(neighbours))

    def ring_copy(ref, way, step, index):
        slot = ring_z(-way * (step - 1))
        src = ref.at[slot] if step > 1 else (k_hbm if ref is k_all else v_hbm)
        return pltpu.make_async_remote_copy(
            src_ref=src,
            dst_ref=ref.at[slot],
            send_sem=ring_send.at[index],
            recv_sem=ring_recv.at[index],
            device_id=z_device(way),
            device_id_type=MESH,
        )

    ring_plan = []
    for ref, way, steps in (
        (k_all, 1, half),
        (v_all, -1, half),
        (v_all, 1, half - 1),
        (k_all, -1, half - 1),
    ):
        ring_plan.append((ref, way, steps))
    ring = {}
    count = 0
    for step in range(1, half + 1):
        for line, (ref, way, steps) in enumerate(ring_plan):
            if step <= steps:
                ring[(line, step)] = ring_copy(ref, way, step, count)
                count += 1
    for line in range(4):
        if (line, 1) in ring:
            ring[(line, 1)].start()

    for way in (1, -1):
        pl.semaphore_signal(
            relay_sem, inc=1, device_id=device(0, 0, way), device_id_type=MESH
        )

    loads = [
        pltpu.make_async_copy(k_hbm, k_all.at[my_z], load_sem.at[0]),
        pltpu.make_async_copy(v_hbm, v_all.at[my_z], load_sem.at[1]),
        pltpu.make_async_copy(g_hbm, g_own, load_sem.at[2]),
        pltpu.make_async_copy(o_hbm, o_own, load_sem.at[3]),
        pltpu.make_async_copy(norm_hbm, norm_own, load_sem.at[4]),
        pltpu.make_async_copy(table_hbm, table, load_sem.at[5]),
        pltpu.make_async_copy(key_order_hbm, key_order, load_sem.at[6]),
        pltpu.make_async_copy(query_order_hbm, query_order, load_sem.at[7]),
    ]
    for copy in loads:
        copy.start()

    def slot_of(sx, sy):
        return (sx + 2 * size_x) % size_x * size_y + (sy + 2 * size_y) % size_y

    def plane_copy(src, dst, sends, receives, tx, ty, sx, sy):
        slot = slot_of(sx - tx, sy - ty)
        pltpu.make_async_remote_copy(
            src_ref=src,
            dst_ref=dst,
            send_sem=sends,
            recv_sem=receives.at[slot],
            device_id=device(0, tx, ty),
            device_id_type=MESH,
        ).start()

    def send_rows(tx, ty):
        group = (my_y + ty + size_y) % size_y
        cols = pl.ds(pl.multiple_of(group * width, 128), width)
        for part, src in enumerate((q_hbm, g_hbm)):
            plane_copy(
                src.at[:, cols],
                qg_all.at[my_rows, pl.ds(part * width, width)],
                qg_send_sem,
                qg_recv_sem,
                tx,
                ty,
                0,
                0,
            )

    def send_nd(tx, ty):
        plane_copy(nd_own, nd_all.at[my_rows], nd_send_sem, nd_recv_sem, tx, ty, 0, 0)

    def wait_chunk(sx, sy):
        at = chunk_rows(sx, sy)
        slot = slot_of(sx, sy)
        pltpu.make_async_copy(qg_all.at[at], qg_all.at[at], qg_recv_sem.at[slot]).wait()
        pltpu.make_async_copy(nd_all.at[at], nd_all.at[at], nd_recv_sem.at[slot]).wait()

    def forward(sx, sy, way):
        at = chunk_rows(sx, sy)
        plane_copy(qg_all.at[at], qg_all.at[at], qg_send_sem, qg_recv_sem, way, 0, sx, sy)
        plane_copy(nd_all.at[at], nd_all.at[at], nd_send_sem, nd_recv_sem, way, 0, sx, sy)

    def ring_step(step):
        for line in range(4):
            if (line, step - 1) in ring:
                ring[(line, step - 1)].wait_recv()
            if (line, step) in ring:
                ring[(line, step)].start()

    beside = ((0, 1), (0, -1), (1, 0), (-1, 0))
    for peer in beside:
        send_rows(*peer)
    own_copies = [
        pltpu.make_async_copy(
            q_hbm.at[:, my_cols], qg_all.at[my_rows, pl.ds(0, width)], own_sem.at[1]
        ),
        pltpu.make_async_copy(
            g_hbm.at[:, my_cols], qg_all.at[my_rows, pl.ds(width, width)], own_sem.at[2]
        ),
    ]
    for copy in own_copies:
        copy.start()

    pl.semaphore_wait(relay_sem, 2)
    for way in (1, -1):
        pl.semaphore_signal(
            relay_x_sem, inc=1, device_id=device(0, way, 0), device_id_type=MESH
        )
    send_rows(0, 2)
    for copy in loads:
        copy.wait()

    lane = lax.broadcasted_iota(jnp.int32, (QCHUNK, 128), 1)
    tile = jnp.zeros((QCHUNK, 128), F32)
    for head in range(heads_all):
        cols = pl.ds(head * HEAD_DIM, HEAD_DIM)
        delta = jnp.sum(
            g_own[:, cols].astype(F32) * o_own[:, cols].astype(F32), axis=1, keepdims=True
        )
        tile = jnp.where(lane == heads_all + head, delta, tile)
    nd_own[...] = tile
    nd_own[:, 0:heads_all] = norm_own[...] * log2e

    for peer in beside:
        send_nd(*peer)
    own_copies.append(pltpu.make_async_copy(nd_own, nd_all.at[my_rows], own_sem.at[0]))
    own_copies[-1].start()
    send_nd(0, 2)

    pl.semaphore_wait(relay_x_sem, 2)
    for tx, ty in ((1, -1), (-1, 1), (-1, 2), (1, 1), (-1, -1), (1, 2)):
        send_rows(tx, ty)
        send_nd(tx, ty)
    ring_step(2)
    if half > 2:
        ring_step(3)
    for sy in (0, 1):
        wait_chunk(-1, sy)
        forward(-1, sy, 1)
    for sy in (-1, 2):
        wait_chunk(1, sy)
        forward(1, sy, -1)
    qlane = lax.broadcasted_iota(jnp.int32, (1, rows), 1)
    qpos = jnp.zeros((1, rows), jnp.int32)
    for chunk in range(plane):
        qpos = jnp.where(qlane // QCHUNK == chunk, query_order[my_z * plane + chunk], qpos)
    offset = key_order.shape[0] * KCHUNK - query_order.shape[0] * QCHUNK
    qpos = offset + qpos * QCHUNK + qlane % QCHUNK
    low = jnp.zeros((1, rows), jnp.int32)
    high = jnp.zeros((1, rows), jnp.int32)
    for row in range(table.shape[1]):
        inside = (qpos >= table[0, row]) & (qpos < table[1, row])
        last = jnp.where(table[4, row] != 0, jnp.minimum(table[3, row], qpos + 1), table[3, row])
        low = jnp.where(inside, table[2, row], low)
        high = jnp.where(inside, last, high)
    krow = lax.broadcasted_iota(jnp.int32, (KCHUNK, rows), 0)
    dq_acc[...] = jnp.zeros_like(dq_acc)

    for step in range(4, half + 1):
        ring_step(step)
    for sy in (1, 2, -1):
        wait_chunk(0, sy)
    for sy in (0, 1):
        wait_chunk(1, sy)
    for sy in (-1, 2):
        wait_chunk(-1, sy)
    for sy in range(size_y):
        wait_chunk(2, sy)
    for copy in own_copies:
        copy.wait()
    turned = nd_all[...].T
    nd_rows[...] = turned[0 : 2 * heads_all]

    order = [0, half]
    for distance in range(half - 1, 0, -1):
        order += [distance, -distance]

    def by_head(first):
        return jnp.concatenate(
            [qg_all[:, pl.ds(first + head * HEAD_DIM, HEAD_DIM)] for head in range(heads_loc)],
            axis=0,
        )

    def block_terms(index, dist):
        zb = ring_z(dist)
        first = (zb * size_x + my_x) * DISPATCH
        for part in range(DISPATCH):
            base = key_order[first + part] * KCHUNK
            ok = (krow >= low - base) & (krow < high - base)
            bias[pl.ds(part * KCHUNK, KCHUNK), :] = jnp.where(ok, jnp.inf, -jnp.inf).astype(F32)
        key_blk = k_all[zb]
        value_blk = v_all[zb]
        weights_low = []
        dscores = []
        for head in range(heads_loc):
            cols = pl.ds(head * HEAD_DIM, HEAD_DIM)
            norm = nd_rows[pl.ds(my_y * heads_loc + head, 1), :]
            delta = nd_rows[pl.ds(heads_all + my_y * heads_loc + head, 1), :]
            scores = dot_nt(key_blk, qg_all[:, cols])
            weights = jnp.exp2(jnp.minimum(scores * (score_scale * log2e) - norm, bias[...]))
            dprobs = dot_nt(value_blk, qg_all[:, pl.ds(width + head * HEAD_DIM, HEAD_DIM)])
            weights_low.append(weights.astype(BF16))
            dscores.append((weights * (dprobs - delta)).astype(BF16))
        part_v[index] = dot_nn(jnp.concatenate(weights_low, axis=1), by_head(width))
        part_k[index] = dot_nn(jnp.concatenate(dscores, axis=1), by_head(0))
        key_turned = key_blk.T
        for head in range(heads_loc):
            dq_acc[:, pl.ds(head * rows, rows)] += dot_nn(key_turned, dscores[head])

    lines = {("k", 1): half, ("v", -1): half, ("v", 1): half - 1, ("k", -1): half - 1}
    slots = {}
    for (kind, way), first_dist in lines.items():
        for dist in range(first_dist, 0, -1):
            slots[(kind, way, dist)] = len(slots)

    def chain_copy(kind, way, dist):
        slot = slots[(kind, way, dist)]
        dst = chain_recv.at[slot]
        if dist == 1:
            dst = (recv_k if kind == "k" else recv_v).at[0 if way == 1 else 1]
        return pltpu.make_async_remote_copy(
            src_ref=chain_send.at[slot],
            dst_ref=dst,
            send_sem=chain_send_sem.at[slot],
            recv_sem=chain_recv_sem.at[slot],
            device_id=z_device(2 * way if dist == half else way),
            device_id_type=MESH,
        )

    def chain_step(kind, way, dist):
        index = order.index(half if dist == half else way * dist)
        value = (part_k if kind == "k" else part_v)[index]
        joined = [dist + 1] if dist < half - 1 else []
        if dist == half - 2 and (kind, way, half) in slots:
            joined.append(half)
        for earlier in joined:
            chain_copy(kind, way, earlier).wait_recv()
            value = value + chain_recv[slots[(kind, way, earlier)]].astype(F32)
        chain_send[slots[(kind, way, dist)]] = value.astype(BF16)
        chain_copy(kind, way, dist).start()

    events = {at: [] for at in range(size_z + 1)}
    events[1] = [("k", 1, 4), ("v", -1, 4)]
    events[2] = [("v", 1, 3)]
    events[3] = [("k", -1, 3), ("k", 1, 3), ("v", -1, 3)]
    events[6] = [("v", 1, 2), ("k", -1, 2)]
    events[7] = [("k", 1, 2), ("v", -1, 2)]
    events[8] = [("v", 1, 1), ("k", -1, 1), ("k", 1, 1), ("v", -1, 1)]

    def dist_at(index):
        near = half - index // 2
        paired = jnp.where(index % 2 == 0, near, -near)
        return jnp.where(index == 0, 0, jnp.where(index == 1, half, paired))

    def block_step(index, carry):
        @pl.when(index == 1)
        def _():
            ring_step(half + 1)

        block_terms(index, dist_at(index))

        for at in range(1, size_z):
            if events[at]:

                @pl.when(index == at)
                def _(at=at):
                    for event in events[at]:
                        chain_step(*event)

        return carry

    lax.fori_loop(0, size_z, block_step, 0, unroll=2)

    stores = [
        pltpu.make_async_copy(part_k.at[0], own_k, store_sem.at[0]),
        pltpu.make_async_copy(part_v.at[0], own_v, store_sem.at[1]),
    ]
    for copy in stores:
        copy.start()

    peers = [(dx, dy) for dx in range(size_x) for dy in range(size_y) if dx or dy]
    peers.sort(key=lambda p: -(min(p[0], size_x - p[0]) + min(p[1], size_y - p[1])))
    for head in range(heads_loc):
        turned = dq_acc[:, pl.ds(head * rows, rows)].T
        dq_send[:, pl.ds(head * HEAD_DIM, HEAD_DIM)] = turned.astype(BF16)
    for dx, dy in peers:
        pltpu.make_async_remote_copy(
            src_ref=dq_send.at[chunk_rows(dx, dy)],
            dst_ref=dq_recv.at[my_x, :, my_cols],
            send_sem=dq_send_sem,
            recv_sem=dq_recv_sem,
            device_id=device(0, dx, dy),
            device_id_type=MESH,
        ).start()
    pltpu.make_async_copy(
        dq_send.at[my_rows], dq_recv.at[my_x, :, my_cols], dq_recv_sem
    ).start()

    for event in events[size_z]:
        chain_step(*event)

    pltpu.make_async_copy(dq_recv, dq_recv, dq_recv_sem).wait()
    for key in slots:
        if key[2] == 1:
            chain_copy(*key).wait_recv()

    for copy in ring.values():
        copy.wait_send()
    for key in slots:
        chain_copy(*key).wait_send()
    sent = pl.ds(0, len(peers) * QCHUNK)
    pltpu.make_async_copy(qg_all.at[sent], qg_all.at[sent], qg_send_sem).wait()
    pltpu.make_async_copy(nd_all.at[sent], nd_all.at[sent], nd_send_sem).wait()
    pltpu.make_async_copy(dq_send.at[sent], dq_send.at[sent], dq_send_sem).wait()
    for copy in stores:
        copy.wait()


def add_up_kernel(dq_recv, own_k, own_v, recv_k, recv_v, dq_out, dk_out, dv_out):
    score_scale = 1.0 / math.sqrt(HEAD_DIM)
    total = dq_recv[0].astype(F32)
    for other in range(1, dq_recv.shape[0]):
        total = total + dq_recv[other].astype(F32)
    dq_out[...] = (total * score_scale).astype(BF16)
    total = own_k[...] + recv_k[0].astype(F32) + recv_k[1].astype(F32)
    dk_out[...] = (total * score_scale).astype(BF16)
    total = own_v[...] + recv_v[0].astype(F32) + recv_v[1].astype(F32)
    dv_out[...] = total.astype(BF16)


def add_up(terms):
    vmem = pl.BlockSpec(memory_space=pltpu.VMEM)
    dq_recv, own_k, own_v = terms[:3]
    return pl.pallas_call(
        add_up_kernel,
        out_shape=(
            jax.ShapeDtypeStruct(dq_recv.shape[1:], BF16),
            jax.ShapeDtypeStruct(own_k.shape, BF16),
            jax.ShapeDtypeStruct(own_v.shape, BF16),
        ),
        in_specs=[vmem] * 5,
        out_specs=(vmem,) * 3,
        name="add_up",
        compiler_params=pltpu.CompilerParams(vmem_limit_bytes=32 * 1024 * 1024),
    )(*(pltpu.with_memory_space_constraint(term, pltpu.VMEM) for term in terms))


def local(
    sizes,
    query_rows,
    key_rows,
    value_rows,
    output_rows,
    grad_out,
    log_norm,
    mask_table,
    key_order,
    query_order,
):
    size_z, size_x, size_y = sizes
    half = size_z // 2
    rows = size_x * size_y * QCHUNK
    key_count = key_rows.shape[0]
    own, columns = query_rows.shape
    heads_all = log_norm.shape[1]
    width = columns // size_y
    chain = 2 * (2 * half - 1)
    hbm = pl.BlockSpec(memory_space=pltpu.HBM)
    dma = pltpu.SemaphoreType.DMA
    terms = pl.pallas_call(
        functools.partial(kernel, sizes),
        out_shape=(
            pltpu.VMEM((size_x,) + query_rows.shape, BF16),
            pltpu.VMEM(key_rows.shape, F32),
            pltpu.VMEM(value_rows.shape, F32),
            pltpu.VMEM((2,) + key_rows.shape, BF16),
            pltpu.VMEM((2,) + value_rows.shape, BF16),
        ),
        in_specs=[hbm] * 9,
        out_specs=(pl.BlockSpec(memory_space=pltpu.VMEM),) * 5,
        scratch_shapes=[
            pltpu.VMEM((rows, 2 * width), BF16),
            pltpu.VMEM((rows, 128), F32),
            pltpu.VMEM((size_z, key_count, HEAD_DIM), BF16),
            pltpu.VMEM((size_z, key_count, HEAD_DIM), BF16),
            pltpu.VMEM((own, columns), BF16),
            pltpu.VMEM((own, columns), BF16),
            pltpu.VMEM((own, heads_all), F32),
            pltpu.VMEM((own, 128), F32),
            pltpu.VMEM((2 * heads_all, rows), F32),
            pltpu.SMEM(mask_table.shape[::-1], jnp.int32),
            pltpu.SMEM(key_order.shape, jnp.int32),
            pltpu.SMEM(query_order.shape, jnp.int32),
            pltpu.VMEM((key_count, rows), F32),
            pltpu.VMEM((HEAD_DIM, width // HEAD_DIM * rows), F32),
            pltpu.VMEM((rows, width), BF16),
            pltpu.VMEM((size_z, key_count, HEAD_DIM), F32),
            pltpu.VMEM((size_z, key_count, HEAD_DIM), F32),
            pltpu.VMEM((chain, key_count, HEAD_DIM), BF16),
            pltpu.VMEM((chain, key_count, HEAD_DIM), BF16),
            dma((8,)),
            dma((3,)),
            pltpu.SemaphoreType.REGULAR,
            pltpu.SemaphoreType.REGULAR,
            dma,
            dma,
            dma((size_x * size_y,)),
            dma((size_x * size_y,)),
            dma((chain,)),
            dma((chain,)),
            dma((chain,)),
            dma((chain,)),
            dma,
            dma,
            dma((2,)),
        ],
        compiler_params=pltpu.CompilerParams(
            collective_id=0, has_side_effects=True, vmem_limit_bytes=32 * 1024 * 1024
        ),
    )(
        *(
            pltpu.with_memory_space_constraint(operand, pltpu.HBM)
            for operand in (
                query_rows,
                key_rows,
                value_rows,
                output_rows,
                grad_out,
                log_norm,
                mask_table.T,
                key_order,
                query_order,
            )
        )
    )
    return add_up(terms)


def solution(mesh, ring_x=RING_X):
    sizes = (mesh.shape["ctx"] // ring_x, ring_x, mesh.shape["head"])
    return jax.shard_map(
        functools.partial(local, sizes),
        mesh=mesh,
        in_specs=(
            P(("dp", "ctx", "head"), None),
            P(("dp", "ctx"), "head"),
            P(("dp", "ctx"), "head"),
            P(("dp", "ctx", "head"), None),
            P(("dp", "ctx", "head"), None),
            P(("dp", "ctx", "head"), None),
            P("dp", None),
            P("dp"),
            P("dp"),
        ),
        out_specs=(
            P(("dp", "ctx", "head"), None),
            P(("dp", "ctx"), "head"),
            P(("dp", "ctx"), "head"),
        ),
        check_vma=False,
    )
```

```python
import functools
import math

import jax
import jax.numpy as jnp
from jax import lax
from jax.experimental import pallas as pl
from jax.experimental.pallas import tpu as pltpu
from jax.sharding import PartitionSpec as P

HEAD_DIM = 128
DISPATCH = 4
KCHUNK = 64
QCHUNK = 16
RING_X = 4
MESH = pl.DeviceIdType.MESH
F32 = jnp.float32
BF16 = jnp.bfloat16


def dot_nt(lhs, rhs):
    return lax.dot_general(lhs, rhs, (((1,), (1,)), ((), ())), preferred_element_type=F32)


def dot_nn(lhs, rhs):
    return lax.dot_general(lhs, rhs, (((1,), (0,)), ((), ())), preferred_element_type=F32)


def kernel(
    sizes,
    q_hbm,
    k_hbm,
    v_hbm,
    o_hbm,
    g_hbm,
    norm_hbm,
    table_hbm,
    key_order_hbm,
    query_order_hbm,
    dq_recv,
    own_k,
    own_v,
    recv_k,
    recv_v,
    qg_all,
    nd_all,
    k_all,
    v_all,
    o_own,
    g_own,
    norm_own,
    nd_own,
    nd_send,
    nd_rows,
    table,
    key_order,
    query_order,
    bias,
    dq_acc,
    dq_send,
    part_k,
    part_v,
    chain_send,
    chain_recv,
    load_sem,
    own_sem,
    relay_sem,
    relay_x_sem,
    qg_send_sem,
    nd_send_sem,
    qg_recv_sem,
    nd_recv_sem,
    ring_send,
    ring_recv,
    chain_send_sem,
    chain_recv_sem,
    dq_send_sem,
    dq_recv_sem,
    store_sem,
):
    size_z, size_x, size_y = sizes
    half = size_z // 2
    plane = size_x * size_y
    rows = plane * QCHUNK
    key_count = k_hbm.shape[0]
    heads_all = norm_hbm.shape[1]
    heads_loc = heads_all // size_y
    width = heads_loc * HEAD_DIM
    score_scale = 1.0 / math.sqrt(HEAD_DIM)
    log2e = math.log2(math.e)

    ctx = lax.axis_index("ctx")
    my_y = lax.axis_index("head")
    my_z = ctx // size_x
    my_x = ctx % size_x
    me = my_x * size_y + my_y
    my_rows = pl.ds(pl.multiple_of(me * QCHUNK, QCHUNK), QCHUNK)
    my_cols = pl.ds(pl.multiple_of(my_y * width, 128), width)

    def ring_z(offset):
        return (my_z + offset + size_z) % size_z

    def device(dz, dx, dy):
        return {
            "ctx": ring_z(dz) * size_x + (my_x + dx + size_x) % size_x,
            "head": (my_y + dy + size_y) % size_y,
        }

    def z_device(offset):
        return device(offset, 0, 0)

    def chunk_rows(sx, sy):
        chunk = (my_x + sx + size_x) % size_x * size_y + (my_y + sy + size_y) % size_y
        return pl.ds(pl.multiple_of(chunk * QCHUNK, QCHUNK), QCHUNK)

    barrier = pltpu.get_barrier_semaphore()
    neighbours = [(1, 0, 0), (-1, 0, 0), (0, 1, 0), (0, -1, 0), (0, 0, 1), (0, 0, -1)]
    for neighbour in neighbours:
        pl.semaphore_signal(
            barrier, inc=1, device_id=device(*neighbour), device_id_type=MESH
        )

    pl.semaphore_wait(barrier, len(neighbours))

    def ring_copy(ref, way, step, index):
        slot = ring_z(-way * (step - 1))
        src = ref.at[slot] if step > 1 else (k_hbm if ref is k_all else v_hbm)
        return pltpu.make_async_remote_copy(
            src_ref=src,
            dst_ref=ref.at[slot],
            send_sem=ring_send.at[index],
            recv_sem=ring_recv.at[index],
            device_id=z_device(way),
            device_id_type=MESH,
        )

    ring_plan = []
    for ref, way, steps in (
        (k_all, 1, half),
        (v_all, -1, half),
        (v_all, 1, half - 1),
        (k_all, -1, half - 1),
    ):
        ring_plan.append((ref, way, steps))
    ring = {}
    count = 0
    for step in range(1, half + 1):
        for line, (ref, way, steps) in enumerate(ring_plan):
            if step <= steps:
                ring[(line, step)] = ring_copy(ref, way, step, count)
                count += 1
    for line in range(4):
        if (line, 1) in ring:
            ring[(line, 1)].start()

    for way in (1, -1):
        pl.semaphore_signal(
            relay_sem, inc=1, device_id=device(0, 0, way), device_id_type=MESH
        )

    loads = [
        pltpu.make_async_copy(k_hbm, k_all.at[my_z], load_sem.at[0]),
        pltpu.make_async_copy(v_hbm, v_all.at[my_z], load_sem.at[1]),
        pltpu.make_async_copy(g_hbm, g_own, load_sem.at[2]),
        pltpu.make_async_copy(o_hbm, o_own, load_sem.at[3]),
        pltpu.make_async_copy(norm_hbm, norm_own, load_sem.at[4]),
        pltpu.make_async_copy(table_hbm, table, load_sem.at[5]),
        pltpu.make_async_copy(key_order_hbm, key_order, load_sem.at[6]),
        pltpu.make_async_copy(query_order_hbm, query_order, load_sem.at[7]),
    ]
    for copy in loads:
        copy.start()

    def slot_of(sx, sy):
        return (sx + 2 * size_x) % size_x * size_y + (sy + 2 * size_y) % size_y

    def plane_copy(src, dst, sends, receives, tx, ty, sx, sy):
        slot = slot_of(sx - tx, sy - ty)
        pltpu.make_async_remote_copy(
            src_ref=src,
            dst_ref=dst,
            send_sem=sends,
            recv_sem=receives.at[slot],
            device_id=device(0, tx, ty),
            device_id_type=MESH,
        ).start()

    def send_rows(tx, ty):
        group = (my_y + ty + size_y) % size_y
        cols = pl.ds(pl.multiple_of(group * width, 128), width)
        for part, src in enumerate((q_hbm, g_hbm)):
            plane_copy(
                src.at[:, cols],
                qg_all.at[my_rows, pl.ds(part * width, width)],
                qg_send_sem,
                qg_recv_sem,
                tx,
                ty,
                0,
                0,
            )

    def send_nd(tx, ty):
        group = (my_y + ty + size_y) % size_y
        plane_copy(
            nd_send.at[group], nd_all.at[my_rows], nd_send_sem, nd_recv_sem, tx, ty, 0, 0
        )

    def wait_chunk(sx, sy):
        at = chunk_rows(sx, sy)
        slot = slot_of(sx, sy)
        pltpu.make_async_copy(qg_all.at[at], qg_all.at[at], qg_recv_sem.at[slot]).wait()
        pltpu.make_async_copy(nd_all.at[at], nd_all.at[at], nd_recv_sem.at[slot]).wait()

    def forward(sx, sy, way):
        at = chunk_rows(sx, sy)
        plane_copy(qg_all.at[at], qg_all.at[at], qg_send_sem, qg_recv_sem, way, 0, sx, sy)
        plane_copy(nd_all.at[at], nd_all.at[at], nd_send_sem, nd_recv_sem, way, 0, sx, sy)

    def ring_step(step):
        for line in range(4):
            if (line, step - 1) in ring:
                ring[(line, step - 1)].wait_recv()
            if (line, step) in ring:
                ring[(line, step)].start()

    beside = ((0, 1), (0, -1), (1, 0), (-1, 0))
    for peer in beside:
        send_rows(*peer)
    own_copies = [
        pltpu.make_async_copy(
            q_hbm.at[:, my_cols], qg_all.at[my_rows, pl.ds(0, width)], own_sem.at[1]
        ),
        pltpu.make_async_copy(
            g_hbm.at[:, my_cols], qg_all.at[my_rows, pl.ds(width, width)], own_sem.at[2]
        ),
    ]
    for copy in own_copies:
        copy.start()

    pl.semaphore_wait(relay_sem, 2)
    for way in (1, -1):
        pl.semaphore_signal(
            relay_x_sem, inc=1, device_id=device(0, way, 0), device_id_type=MESH
        )
    send_rows(0, 2)
    pl.semaphore_wait(relay_x_sem, 2)
    passed_on = ((1, -1), (-1, 1), (-1, 2), (1, 1), (-1, -1), (1, 2))
    for peer in passed_on:
        send_rows(*peer)
    for copy in loads:
        copy.wait()

    lane = lax.broadcasted_iota(jnp.int32, (QCHUNK, 128), 1)
    tile = jnp.zeros((QCHUNK, 128), F32)
    for head in range(heads_all):
        cols = pl.ds(head * HEAD_DIM, HEAD_DIM)
        delta = jnp.sum(
            g_own[:, cols].astype(F32) * o_own[:, cols].astype(F32), axis=1, keepdims=True
        )
        tile = jnp.where(lane == heads_all + head, delta, tile)
    nd_own[...] = tile
    nd_own[:, 0:heads_all] = jnp.clip(norm_own[...] * log2e, -1e30, 1e30)
    both = nd_own[...]
    for group in range(size_y):
        first = group * heads_loc
        norms = pltpu.roll(both, (128 - first) % 128, 1)
        deltas = pltpu.roll(both, (128 - heads_all - first + heads_loc) % 128, 1)
        value = jnp.where(
            lane < heads_loc, norms, jnp.where(lane < 2 * heads_loc, deltas, 0.0)
        )
        packed = jnp.zeros_like(value)
        for term in range(3):
            rounded = value.astype(BF16).astype(F32)
            value = value - rounded
            packed = packed + (pltpu.roll(rounded, 16 * term, 1) if term else rounded)
        nd_send[group] = packed.astype(BF16)

    for peer in beside:
        send_nd(*peer)
    own_copies.append(pltpu.make_async_copy(nd_send.at[my_y], nd_all.at[my_rows], own_sem.at[0]))
    own_copies[-1].start()
    for peer in passed_on:
        send_nd(*peer)
    send_nd(0, 2)

    ring_step(2)
    if half > 2:
        ring_step(3)
    for sy in (0, 1):
        wait_chunk(-1, sy)
        forward(-1, sy, 1)
    for sy in (-1, 2):
        wait_chunk(1, sy)
        forward(1, sy, -1)
    qlane = lax.broadcasted_iota(jnp.int32, (1, rows), 1)
    qpos = jnp.zeros((1, rows), jnp.int32)
    for chunk in range(plane):
        qpos = jnp.where(qlane // QCHUNK == chunk, query_order[my_z * plane + chunk], qpos)
    offset = key_order.shape[0] * KCHUNK - query_order.shape[0] * QCHUNK
    qpos = offset + qpos * QCHUNK + qlane % QCHUNK
    low = jnp.zeros((1, rows), jnp.int32)
    high = jnp.zeros((1, rows), jnp.int32)
    for row in range(table.shape[1]):
        inside = (qpos >= table[0, row]) & (qpos < table[1, row])
        last = jnp.where(table[4, row] != 0, jnp.minimum(table[3, row], qpos + 1), table[3, row])
        low = jnp.where(inside, table[2, row], low)
        high = jnp.where(inside, last, high)
    krow = lax.broadcasted_iota(jnp.int32, (KCHUNK, rows), 0)
    dq_acc[...] = jnp.zeros_like(dq_acc)

    for step in range(4, half + 1):
        ring_step(step)
    for sy in (1, 2, -1):
        wait_chunk(0, sy)
    for sy in (0, 1):
        wait_chunk(1, sy)
    for sy in (-1, 2):
        wait_chunk(-1, sy)
    for sy in range(size_y):
        wait_chunk(2, sy)
    for copy in own_copies:
        copy.wait()
    turned = nd_all[...].astype(F32).T
    nd_rows[...] = turned[0:16] + turned[16:32] + turned[32:48]

    order = [0, half]
    for distance in range(half - 1, 0, -1):
        order += [distance, -distance]

    def by_head(first):
        return jnp.concatenate(
            [qg_all[:, pl.ds(first + head * HEAD_DIM, HEAD_DIM)] for head in range(heads_loc)],
            axis=0,
        )

    def block_terms(index, dist):
        zb = ring_z(dist)
        first = (zb * size_x + my_x) * DISPATCH
        for part in range(DISPATCH):
            base = key_order[first + part] * KCHUNK
            ok = (krow >= low - base) & (krow < high - base)
            bias[pl.ds(part * KCHUNK, KCHUNK), :] = jnp.where(ok, jnp.inf, -jnp.inf).astype(F32)
        key_blk = k_all[zb]
        value_blk = v_all[zb]
        weights_low = []
        dscores = []
        for head in range(heads_loc):
            cols = pl.ds(head * HEAD_DIM, HEAD_DIM)
            norm = nd_rows[pl.ds(head, 1), :]
            delta = nd_rows[pl.ds(heads_loc + head, 1), :]
            scores = dot_nt(key_blk, qg_all[:, cols])
            weights = jnp.exp2(jnp.minimum(scores * (score_scale * log2e) - norm, bias[...]))
            dprobs = dot_nt(value_blk, qg_all[:, pl.ds(width + head * HEAD_DIM, HEAD_DIM)])
            weights_low.append(weights.astype(BF16))
            dscores.append((weights * (dprobs - delta)).astype(BF16))
        part_v[index] = dot_nn(jnp.concatenate(weights_low, axis=1), by_head(width))
        part_k[index] = dot_nn(jnp.concatenate(dscores, axis=1), by_head(0))
        key_turned = key_blk.T
        for head in range(heads_loc):
            dq_acc[:, pl.ds(head * rows, rows)] += dot_nn(key_turned, dscores[head])

    lines = {("k", 1): half, ("v", -1): half, ("v", 1): half - 1, ("k", -1): half - 1}
    slots = {}
    for (kind, way), first_dist in lines.items():
        for dist in range(first_dist, 0, -1):
            slots[(kind, way, dist)] = len(slots)

    def chain_copy(kind, way, dist):
        slot = slots[(kind, way, dist)]
        dst = chain_recv.at[slot]
        if dist == 1:
            dst = (recv_k if kind == "k" else recv_v).at[0 if way == 1 else 1]
        return pltpu.make_async_remote_copy(
            src_ref=chain_send.at[slot],
            dst_ref=dst,
            send_sem=chain_send_sem.at[slot],
            recv_sem=chain_recv_sem.at[slot],
            device_id=z_device(2 * way if dist == half else way),
            device_id_type=MESH,
        )

    def chain_step(kind, way, dist):
        index = order.index(half if dist == half else way * dist)
        value = (part_k if kind == "k" else part_v)[index]
        joined = [dist + 1] if dist < half - 1 else []
        if dist == half - 2 and (kind, way, half) in slots:
            joined.append(half)
        for earlier in joined:
            chain_copy(kind, way, earlier).wait_recv()
            value = value + chain_recv[slots[(kind, way, earlier)]].astype(F32)
        chain_send[slots[(kind, way, dist)]] = value.astype(BF16)
        chain_copy(kind, way, dist).start()

    events = {at: [] for at in range(size_z + 1)}
    events[1] = [("k", 1, 4), ("v", -1, 4)]
    events[2] = [("v", 1, 3)]
    events[3] = [("k", -1, 3), ("k", 1, 3), ("v", -1, 3)]
    events[6] = [("v", 1, 2), ("k", -1, 2)]
    events[7] = [("k", 1, 2), ("v", -1, 2)]
    events[8] = [("v", 1, 1), ("k", -1, 1), ("k", 1, 1), ("v", -1, 1)]

    def dist_at(index):
        near = half - index // 2
        paired = jnp.where(index % 2 == 0, near, -near)
        return jnp.where(index == 0, 0, jnp.where(index == 1, half, paired))

    def block_step(index, carry):
        @pl.when(index == 1)
        def _():
            ring_step(half + 1)

        block_terms(index, dist_at(index))

        for at in range(1, size_z):
            if events[at]:

                @pl.when(index == at)
                def _(at=at):
                    for event in events[at]:
                        chain_step(*event)

        return carry

    lax.fori_loop(0, size_z, block_step, 0, unroll=2)

    stores = [
        pltpu.make_async_copy(part_k.at[0], own_k, store_sem.at[0]),
        pltpu.make_async_copy(part_v.at[0], own_v, store_sem.at[1]),
    ]
    for copy in stores:
        copy.start()

    peers = [(dx, dy) for dx in range(size_x) for dy in range(size_y) if dx or dy]
    peers.sort(key=lambda p: -(min(p[0], size_x - p[0]) + min(p[1], size_y - p[1])))
    for head in range(heads_loc):
        turned = dq_acc[:, pl.ds(head * rows, rows)].T
        dq_send[:, pl.ds(head * HEAD_DIM, HEAD_DIM)] = turned.astype(BF16)
    for dx, dy in peers:
        pltpu.make_async_remote_copy(
            src_ref=dq_send.at[chunk_rows(dx, dy)],
            dst_ref=dq_recv.at[my_x, :, my_cols],
            send_sem=dq_send_sem,
            recv_sem=dq_recv_sem,
            device_id=device(0, dx, dy),
            device_id_type=MESH,
        ).start()
    pltpu.make_async_copy(
        dq_send.at[my_rows], dq_recv.at[my_x, :, my_cols], dq_recv_sem
    ).start()

    for event in events[size_z]:
        chain_step(*event)

    pltpu.make_async_copy(dq_recv, dq_recv, dq_recv_sem).wait()
    for key in slots:
        if key[2] == 1:
            chain_copy(*key).wait_recv()

    for copy in ring.values():
        copy.wait_send()
    for key in slots:
        chain_copy(*key).wait_send()
    sent = pl.ds(0, len(peers) * QCHUNK)
    pltpu.make_async_copy(qg_all.at[sent], qg_all.at[sent], qg_send_sem).wait()
    pltpu.make_async_copy(nd_all.at[sent], nd_all.at[sent], nd_send_sem).wait()
    pltpu.make_async_copy(dq_send.at[sent], dq_send.at[sent], dq_send_sem).wait()
    for copy in stores:
        copy.wait()


def add_up_kernel(dq_recv, own_k, own_v, recv_k, recv_v, dq_out, dk_out, dv_out):
    score_scale = 1.0 / math.sqrt(HEAD_DIM)
    total = dq_recv[0].astype(F32)
    for other in range(1, dq_recv.shape[0]):
        total = total + dq_recv[other].astype(F32)
    dq_out[...] = (total * score_scale).astype(BF16)
    total = own_k[...] + recv_k[0].astype(F32) + recv_k[1].astype(F32)
    dk_out[...] = (total * score_scale).astype(BF16)
    total = own_v[...] + recv_v[0].astype(F32) + recv_v[1].astype(F32)
    dv_out[...] = total.astype(BF16)


def add_up(terms):
    vmem = pl.BlockSpec(memory_space=pltpu.VMEM)
    dq_recv, own_k, own_v = terms[:3]
    return pl.pallas_call(
        add_up_kernel,
        out_shape=(
            jax.ShapeDtypeStruct(dq_recv.shape[1:], BF16),
            jax.ShapeDtypeStruct(own_k.shape, BF16),
            jax.ShapeDtypeStruct(own_v.shape, BF16),
        ),
        in_specs=[vmem] * 5,
        out_specs=(vmem,) * 3,
        name="add_up",
        compiler_params=pltpu.CompilerParams(vmem_limit_bytes=32 * 1024 * 1024),
    )(*(pltpu.with_memory_space_constraint(term, pltpu.VMEM) for term in terms))


def local(
    sizes,
    query_rows,
    key_rows,
    value_rows,
    output_rows,
    grad_out,
    log_norm,
    mask_table,
    key_order,
    query_order,
):
    size_z, size_x, size_y = sizes
    half = size_z // 2
    rows = size_x * size_y * QCHUNK
    key_count = key_rows.shape[0]
    own, columns = query_rows.shape
    heads_all = log_norm.shape[1]
    width = columns // size_y
    chain = 2 * (2 * half - 1)
    hbm = pl.BlockSpec(memory_space=pltpu.HBM)
    dma = pltpu.SemaphoreType.DMA
    terms = pl.pallas_call(
        functools.partial(kernel, sizes),
        out_shape=(
            pltpu.VMEM((size_x,) + query_rows.shape, BF16),
            pltpu.VMEM(key_rows.shape, F32),
            pltpu.VMEM(value_rows.shape, F32),
            pltpu.VMEM((2,) + key_rows.shape, BF16),
            pltpu.VMEM((2,) + value_rows.shape, BF16),
        ),
        in_specs=[hbm] * 9,
        out_specs=(pl.BlockSpec(memory_space=pltpu.VMEM),) * 5,
        scratch_shapes=[
            pltpu.VMEM((rows, 2 * width), BF16),
            pltpu.VMEM((rows, 128), BF16),
            pltpu.VMEM((size_z, key_count, HEAD_DIM), BF16),
            pltpu.VMEM((size_z, key_count, HEAD_DIM), BF16),
            pltpu.VMEM((own, columns), BF16),
            pltpu.VMEM((own, columns), BF16),
            pltpu.VMEM((own, heads_all), F32),
            pltpu.VMEM((own, 128), F32),
            pltpu.VMEM((size_y, own, 128), BF16),
            pltpu.VMEM((16, rows), F32),
            pltpu.SMEM(mask_table.shape[::-1], jnp.int32),
            pltpu.SMEM(key_order.shape, jnp.int32),
            pltpu.SMEM(query_order.shape, jnp.int32),
            pltpu.VMEM((key_count, rows), F32),
            pltpu.VMEM((HEAD_DIM, width // HEAD_DIM * rows), F32),
            pltpu.VMEM((rows, width), BF16),
            pltpu.VMEM((size_z, key_count, HEAD_DIM), F32),
            pltpu.VMEM((size_z, key_count, HEAD_DIM), F32),
            pltpu.VMEM((chain, key_count, HEAD_DIM), BF16),
            pltpu.VMEM((chain, key_count, HEAD_DIM), BF16),
            dma((8,)),
            dma((3,)),
            pltpu.SemaphoreType.REGULAR,
            pltpu.SemaphoreType.REGULAR,
            dma,
            dma,
            dma((size_x * size_y,)),
            dma((size_x * size_y,)),
            dma((chain,)),
            dma((chain,)),
            dma((chain,)),
            dma((chain,)),
            dma,
            dma,
            dma((2,)),
        ],
        compiler_params=pltpu.CompilerParams(
            collective_id=0, has_side_effects=True, vmem_limit_bytes=32 * 1024 * 1024
        ),
    )(
        *(
            pltpu.with_memory_space_constraint(operand, pltpu.HBM)
            for operand in (
                query_rows,
                key_rows,
                value_rows,
                output_rows,
                grad_out,
                log_norm,
                mask_table.T,
                key_order,
                query_order,
            )
        )
    )
    return add_up(terms)


def solution(mesh, ring_x=RING_X):
    sizes = (mesh.shape["ctx"] // ring_x, ring_x, mesh.shape["head"])
    return jax.shard_map(
        functools.partial(local, sizes),
        mesh=mesh,
        in_specs=(
            P(("dp", "ctx", "head"), None),
            P(("dp", "ctx"), "head"),
            P(("dp", "ctx"), "head"),
            P(("dp", "ctx", "head"), None),
            P(("dp", "ctx", "head"), None),
            P(("dp", "ctx", "head"), None),
            P("dp", None),
            P("dp"),
            P("dp"),
        ),
        out_specs=(
            P(("dp", "ctx", "head"), None),
            P(("dp", "ctx"), "head"),
            P(("dp", "ctx"), "head"),
        ),
        check_vma=False,
    )
```
